32 devices in a mesh: pipe: 4 (over y, core), req: 2 (over x), tp: 4 (over z).
Axes of the slice: x: 2, y: 2, z: 4, core: 2. Of those that a mesh axis runs over, the one named last changes fastest.
Arguments:
- hidden: bfloat16 [256, 8192], P('req', 'tp'), may hold values from -64 to 64
- queries: bfloat16 [4, 256, 4096], P('pipe', 'req', 'tp'), may hold values from -32 to 32
- norm_gain: bfloat16 [4, 8192], P('pipe'), may hold values from 0.5 to 1.5
- kv_weight: bfloat16 [4, 8192, 2, 512], P('pipe', None, None, 'tp'), may hold values from -0.0625 to 0.0625
- adapter_in: bfloat16 [4, 8, 64, 4096], P('pipe', 'req', None, 'tp'), may hold values from -0.09375 to 0.09375
- adapter_out: bfloat16 [4, 8, 64, 8192], P('pipe', 'req', None, 'tp'), may hold values from -3 to 3
- kv_pages: bfloat16 [4, 256, 2, 64, 512], P('pipe', 'req', None, None, 'tp'), may hold values from -4 to 4
- adapter_ids: int32 [64], P('req'), may hold values from 0 to 7, as said below
- owner_rows: int32 [8], replicated, may hold values from 0 to 7, as said below
- page_table: int32 [64, 4], P('req'), may hold values from 0 to 127, as said below
- lengths: int32 [64], P('req'), may hold values from 1 to 252, as said below
- moves: int32 [32, 3], P('req'), may hold values from 0 to 127, as said below
Outputs:
- section_out: bfloat16 [4, 256, 8192], P('pipe', 'req', 'tp')
- new_kv: bfloat16 [4, 256, 2, 512], P('pipe', 'req', None, 'tp')
- arrived: bfloat16 [4, 32, 2, 64, 512], P('pipe', 'req', None, None, 'tp')
The draws below stay inside these ranges and needn't reach their ends.
Inputs may be any that keep to these rules, and one draw needn't show every extreme that they name: `adapter_ids`: adapter a is stored at row owner_rows[a], on request device owner_rows[a] // 4. In each aligned block of 16 requests at most 16 requests have adapters stored on one request device, and in every block some device stores exactly 16 of them. `owner_rows`: each storage row once. `page_table`: the 128 slots of one request device are each named once by its requests. `lengths`: every request device has a request of length 252. `moves`: row i * 16 + k belongs to request device i. Its destination differs from i; its source slots are distinct; at most 16 of its rows name one destination, exactly 16 for some; destination slots are below 16 and distinct among all rows that name one destination.
All inputs are finite; a program needn't handle non-finite values.
Results may differ from the reference program's by a relative error of at most 0.02.
Values may be sent and summed in bfloat16 or wider, within the bound.
No kernel may reach another device: no remote copies, remote signals or barrier semaphores. Data moves between devices by JAX's collectives and lax.ppermute only.
A program may use at most 128 MiB of HBM per device.

```python
import math
import jax
import jax.numpy as jnp
from jax import lax

D = 8192
HD = 128
QH = 32
KVH = 4
R = 64
ADP_DEV = 4
RQ = 32
S = 4
PAGE = 64
MAXP = 4
MOVES = 16
LAYERS = 4
REQUESTS = 64
TOKENS = 256
ADAPTERS = 8
RQ_MB = 16
CTX = 256
USED = 128
POOL_ALL = 256
MOVES_ALL = 32
FREE = 16
FREE_ALL = 32


def owner_perm(key):
    return jax.random.permutation(jax.random.fold_in(key, 11), ADAPTERS).astype(jnp.int32)


def draw_owner_rows(key, part):
    return owner_perm(key)


def draw_adapter_ids(key, part):
    req_count = REQUESTS // RQ
    block_count = REQUESTS // RQ_MB
    block_cap = min(RQ_MB, max(2, 2 * RQ_MB // req_count))
    slot_total = req_count * block_cap
    inverse = jnp.argsort(owner_perm(key)).astype(jnp.int32)
    seed_key = jax.random.fold_in(key, 12)

    def one_block(block_id):
        block_key = jax.random.fold_in(seed_key, block_id)
        key_full, key_score, key_order, key_local = jax.random.split(block_key, 4)
        full_dest = jax.random.randint(key_full, (), 0, req_count)
        slot_ids = jnp.arange(slot_total, dtype=jnp.int32)
        dest_of = slot_ids // block_cap
        scores = jax.random.randint(key_score, (slot_total,), 0, 1 << 20) * slot_total + slot_ids
        scores = jnp.where(dest_of == full_dest, slot_ids - slot_total, scores)
        picked = dest_of[jnp.argsort(scores)[:RQ_MB]]
        picked = picked[jax.random.permutation(key_order, RQ_MB)]
        local_row = jax.random.randint(key_local, (RQ_MB,), 0, ADP_DEV)
        return inverse[picked * ADP_DEV + local_row]
    return jax.vmap(one_block)(jnp.arange(block_count, dtype=jnp.int32)).reshape(REQUESTS).astype(jnp.int32)


def draw_page_table(key, part):
    req_count = REQUESTS // RQ
    key_list = jax.random.split(jax.random.fold_in(key, 31), req_count)
    tables = jax.vmap(lambda one_key: jax.random.permutation(one_key, USED))(key_list)
    return tables.reshape(REQUESTS, MAXP).astype(jnp.int32)


def draw_lengths(key, part):
    req_count = REQUESTS // RQ
    drawn = jax.random.randint(jax.random.fold_in(key, 21), (req_count, RQ), 1, CTX - S + 1)
    longest = jax.random.randint(jax.random.fold_in(key, 22), (req_count, 1), 0, RQ)
    filled = jnp.where(jnp.arange(RQ, dtype=jnp.int32)[None, :] == longest, CTX - S, drawn)
    return filled.reshape(REQUESTS).astype(jnp.int32)


def draw_moves(key, part):
    req_count = REQUESTS // RQ
    span_len = req_count - 1
    cap_pair = (MOVES + req_count - 2) // span_len
    shifts = jax.random.randint(jax.random.fold_in(key, 41), (req_count, 1), 0, span_len)
    source = jnp.arange(req_count, dtype=jnp.int32)[:, None]
    moving = jnp.arange(MOVES, dtype=jnp.int32)[None, :]
    offsets = (moving + shifts) % span_len
    target = (source + 1 + offsets) % req_count
    serial = moving // span_len
    distance = (source - target) % req_count
    landing = (distance - 1) * cap_pair + serial
    key_list = jax.random.split(jax.random.fold_in(key, 42), req_count)
    src_slots = jax.vmap(lambda one_key: jax.random.permutation(one_key, USED)[:MOVES])(key_list)
    return jnp.stack([target, src_slots, landing], axis=-1).reshape(MOVES_ALL, 3).astype(jnp.int32)


def draw_kv_pages(key, part):
    full_shape = (LAYERS, POOL_ALL, 2, PAGE, KVH * HD)
    values = jnp.clip(jax.random.normal(jax.random.fold_in(key, 62), full_shape, jnp.float32), -4.0, 4.0)
    part_scale = jnp.array([0.5, 1.0], jnp.float32).reshape(1, 1, 2, 1, 1)
    values = values * part_scale
    return values.astype(jnp.bfloat16)


def draw_queries(key, part):
    full_shape = (LAYERS, TOKENS, QH * HD)
    values = jnp.clip(2.0 * jax.random.normal(jax.random.fold_in(key, 72), full_shape, jnp.float32), -8.0, 8.0)
    return values.astype(jnp.bfloat16)


def draw_hidden(key, part):
    row_scale = jnp.exp(jax.random.uniform(jax.random.fold_in(key, 82), (TOKENS, 1), jnp.float32, math.log(0.4), math.log(4.0)))
    col_scale = jnp.exp(jax.random.uniform(jax.random.fold_in(key, 83), (1, D), jnp.float32, math.log(0.4), math.log(4.0)))
    base_vals = jnp.clip(jax.random.normal(jax.random.fold_in(key, 85), (TOKENS, D), jnp.float32), -4.0, 4.0)
    return (base_vals * row_scale * col_scale).astype(jnp.bfloat16)


def levels(key, shape, shards, least, largest):
    level = 1.0
    for position, blocks in shards:
        steps = jax.random.uniform(jax.random.fold_in(jax.random.fold_in(key, 6), position), (blocks,), jnp.float32, least / len(shards), largest / len(shards))
        level = level * jnp.repeat(jnp.exp(steps), shape[position] // blocks).reshape((-1,) + (1,) * (len(shape) - 1 - position))
    return level


def scatter_about(key, shape, deviation, reach, cuts=(), kind=jnp.bfloat16):
    values = deviation * jax.random.normal(key, shape, jnp.float32)
    if cuts:
        values = values * levels(key, shape, cuts, -0.22, 0.18)
    return jnp.clip(values, -reach, reach).astype(kind)


def setup_inputs(seed: int = 0) -> dict:
    splits = jax.random.split(jax.random.key(seed), 13)
    return {
        "hidden": draw_hidden(jax.random.fold_in(splits[12], 71), 0),
        "queries": draw_queries(jax.random.fold_in(splits[12], 71), 0),
        "norm_gain": jnp.clip(1.0 + 0.1 * jax.random.normal(splits[2], (LAYERS, D), jnp.float32), 0.5, 1.5).astype(jnp.bfloat16),
        "kv_weight": scatter_about(splits[3], (LAYERS, D, 2, KVH * HD), D ** -0.5, 0.0625, ((0, 4), (3, 4))),
        "adapter_in": scatter_about(splits[4], (LAYERS, ADAPTERS, R, QH * HD), (QH * HD) ** -0.5, 0.09375, ((0, 4), (1, 2), (3, 4))),
        "adapter_out": scatter_about(splits[5], (LAYERS, ADAPTERS, R, D), (R // 16) ** -0.5, 3.0, ((0, 4), (1, 2), (3, 4))),
        "kv_pages": draw_kv_pages(jax.random.fold_in(splits[12], 71), 0),
        "adapter_ids": draw_adapter_ids(jax.random.fold_in(splits[12], 71), 0),
        "owner_rows": draw_owner_rows(jax.random.fold_in(splits[12], 71), 0),
        "page_table": draw_page_table(jax.random.fold_in(splits[12], 71), 0),
        "lengths": draw_lengths(jax.random.fold_in(splits[12], 71), 0),
        "moves": draw_moves(jax.random.fold_in(splits[12], 71), 0),
    }


def rotate(key_vecs, positions):
    half_dim = key_vecs.shape[-1] // 2
    inv_freq = jnp.exp(-math.log(500000.0) * (2.0 * jnp.arange(half_dim, dtype=jnp.float32) / key_vecs.shape[-1]))
    angles = positions.astype(jnp.float32)[..., None, None] * inv_freq
    cos_vals = jnp.cos(angles)
    sin_vals = jnp.sin(angles)
    front_half = key_vecs[..., :half_dim]
    back_half = key_vecs[..., half_dim:]
    return jnp.concatenate([front_half * cos_vals - back_half * sin_vals, back_half * cos_vals + front_half * sin_vals], axis=-1)

def reference(hidden, queries, norm_gain, kv_weight, adapter_in, adapter_out, kv_pages, adapter_ids, owner_rows, page_table, lengths, moves):
    group_size = QH // KVH
    token_ids = jnp.arange(S, dtype=jnp.int32)
    device_base = jnp.arange(REQUESTS, dtype=jnp.int32) // RQ * USED
    global_table = page_table + device_base[:, None]
    positions = (lengths[:, None] + token_ids[None, :]).reshape(TOKENS)
    page_slot = jnp.take_along_axis(global_table, (positions // PAGE).reshape(REQUESTS, S), axis=1).reshape(TOKENS)
    page_offset = positions % PAGE
    store_rows = owner_rows[adapter_ids]
    source_dev = jnp.arange(MOVES_ALL, dtype=jnp.int32) // MOVES
    key_index = jnp.arange(CTX + S, dtype=jnp.int32)
    hstate = hidden
    section_list = []
    fresh_list = []
    arrived_list = []
    for layer_id in range(LAYERS):
        widened = hstate.astype(jnp.float32)
        inv_rms = lax.rsqrt(lax.optimization_barrier(jnp.mean(widened * widened, axis=-1, keepdims=True)) + 1e-05)
        normed = (widened * inv_rms * norm_gain[layer_id].astype(jnp.float32)).astype(jnp.bfloat16)
        projected = jnp.dot(normed, kv_weight[layer_id].reshape(D, 2 * KVH * HD), preferred_element_type=jnp.float32).reshape(TOKENS, 2, KVH, HD)
        new_keys = rotate(projected[:, 0], positions).astype(jnp.bfloat16)
        new_values = projected[:, 1].astype(jnp.bfloat16)
        fresh_kv = jnp.stack([new_keys, new_values], axis=1).reshape(TOKENS, 2, KVH * HD)
        layer_pages = kv_pages[layer_id]

        def attend_one(inputs):
            page_rows, length, query_req, fresh_req = inputs
            gathered = layer_pages[page_rows]
            cached = jnp.swapaxes(gathered, 0, 1).reshape(2, CTX, KVH, HD)
            fresh_heads = fresh_req.reshape(S, 2, KVH, HD)
            key_all = jnp.concatenate([cached[0], fresh_heads[:, 0]], axis=0).astype(jnp.float32)
            value_all = jnp.concatenate([cached[1], fresh_heads[:, 1]], axis=0).astype(jnp.float32)
            query_heads = query_req.reshape(S, KVH, group_size, HD).astype(jnp.float32)
            scores = jnp.einsum('skgd,tkd->skgt', query_heads, key_all) * HD ** (-0.5)
            allowed = jnp.where(key_index[None, :] < CTX, key_index[None, :] < length, key_index[None, :] - CTX <= token_ids[:, None])
            scores = jnp.where(allowed[:, None, None, :], scores, -jnp.inf)
            row_max = lax.optimization_barrier(jnp.max(scores, axis=-1, keepdims=True))
            exp_scores = jnp.exp(scores - row_max)
            weights = (exp_scores / lax.optimization_barrier(jnp.sum(exp_scores, axis=-1, keepdims=True))).astype(jnp.bfloat16)
            mixed = jnp.einsum('skgt,tkd->skgd', weights.astype(jnp.float32), value_all)
            return mixed.reshape(S, QH * HD).astype(jnp.bfloat16)
        attended = lax.map(attend_one, (global_table, lengths, queries[layer_id].reshape(REQUESTS, S, QH * HD), fresh_kv.reshape(REQUESTS, S, 2 * KVH * HD)))

        def adapt_one(inputs):
            store_row, attended_req = inputs
            rank_low = jnp.dot(attended_req, adapter_in[layer_id, store_row].T, preferred_element_type=jnp.float32).astype(jnp.bfloat16)
            return jnp.dot(rank_low, adapter_out[layer_id, store_row], preferred_element_type=jnp.float32).astype(jnp.bfloat16)
        deltas = lax.map(adapt_one, (store_rows, attended)).reshape(TOKENS, D)
        hstate = (hstate.astype(jnp.float32) + deltas.astype(jnp.float32)).astype(jnp.bfloat16)
        section_list.append(hstate)
        fresh_list.append(fresh_kv)
        written = layer_pages.at[page_slot, :, page_offset, :].set(fresh_kv)
        leaving = written[source_dev * USED + moves[:, 1]]
        empty_pages = jnp.zeros((FREE_ALL, 2, PAGE, KVH * HD), jnp.bfloat16)
        arrived_list.append(empty_pages.at[moves[:, 0] * FREE + moves[:, 2]].set(leaving))
    return (jnp.stack(section_list), jnp.stack(fresh_list), jnp.stack(arrived_list))
```

```python
import functools
import math

import jax
import jax.numpy as jnp
from jax import lax
from jax.experimental import pallas as pl
from jax.experimental.pallas import tpu as pltpu
from jax.sharding import PartitionSpec as P

HD = 128
R = 64
S = 4
PAGE = 64
MAXP = 4
EPS = 1e-05
BIG = -1e30
SCALE = HD ** (-0.5)
VM = pl.BlockSpec(memory_space=pltpu.VMEM)
SM = pl.BlockSpec(memory_space=pltpu.SMEM)
ANY = pl.BlockSpec(memory_space=pl.ANY)
NT = (((1,), (1,)), ((), ()))


def params(mib):
    return pltpu.CompilerParams(vmem_limit_bytes=mib << 20)


def sds(shape, dtype):
    return jax.ShapeDtypeStruct(shape, dtype)


def halves_of(rows):
    return rows // 2


def split_parts_kernel(raw_ref, out_ref, wide):
    wide[...] = raw_ref[...].astype(jnp.float32)
    rows = out_ref.shape[0]
    out_ref[:, :HD] = wide[pl.ds(0, rows, stride=2), :].astype(jnp.bfloat16)
    out_ref[:, HD:] = wide[pl.ds(1, rows, stride=2), :].astype(jnp.bfloat16)


def split_parts(raw):
    rows = raw.shape[0] // 2
    step = 1024
    return pl.pallas_call(
        split_parts_kernel,
        grid=(rows // step,),
        in_specs=[pl.BlockSpec((2 * step, HD), lambda i: (i, 0))],
        out_specs=pl.BlockSpec((step, 2 * HD), lambda i: (i, 0)),
        out_shape=sds((rows, 2 * HD), jnp.bfloat16),
        scratch_shapes=[pltpu.VMEM((2 * step, HD), jnp.float32)],
        compiler_params=params(16),
        name="split_parts",
    )(raw)


def cached_kernel(table_ref, len_ref, q_ref, pages_ref, acc_ref, lse_ref, buf, wide_q, sems):
    heads = acc_ref.shape[0]
    reqs = len_ref.shape[0]
    per = 8 // S
    ctx = MAXP * PAGE
    pages = per * MAXP

    def start(i, _):
        pltpu.make_async_copy(
            pages_ref.at[table_ref[i]], buf.at[i], sems.at[i // pages]
        ).start()
        return 0

    lax.fori_loop(0, reqs * MAXP, start, 0)
    wide_q[...] = q_ref[...].astype(jnp.float32)
    shape = (heads * 8, per * ctx)
    rows = lax.broadcasted_iota(jnp.int32, shape, 0)
    cols = lax.broadcasted_iota(jnp.int32, shape, 1)
    own = (rows % 8) // S == cols // ctx
    at = jnp.where(own, cols % ctx, 2 * ctx)
    second = cols >= ctx
    lanes = lax.broadcasted_iota(jnp.int32, (8, HD), 1)

    def group(g, _):
        first = pl.multiple_of(g * pages, pages)
        block = buf.at[pl.ds(first, pages)]
        pltpu.make_async_copy(block, block, sems.at[g]).wait()
        row = pl.multiple_of(g * 8, 8)
        q = jnp.concatenate(
            [wide_q[pl.ds(row, 8), h * HD : (h + 1) * HD] for h in range(heads)], axis=0
        ).astype(jnp.bfloat16)
        keys = buf[pl.ds(first, pages), 0].reshape(per * ctx, HD)
        values = buf[pl.ds(first, pages), 1].reshape(per * ctx, HD)
        scores = lax.dot_general(q, keys, NT, preferred_element_type=jnp.float32) * SCALE
        limit = jnp.where(second, len_ref[g * per + 1], len_ref[g * per])
        scores = jnp.where(at < limit, scores, BIG)
        top = jnp.max(scores, axis=1, keepdims=True)
        weights = jnp.exp(scores - top)
        total = jnp.sum(weights, axis=1, keepdims=True)
        mixed = jnp.dot(weights.astype(jnp.bfloat16), values, preferred_element_type=jnp.float32)
        mixed = mixed / total
        lse = top + jnp.log(total)
        packed = jnp.zeros((8, HD), jnp.float32)
        for h in range(heads):
            acc_ref[h, pl.ds(row, 8), :] = mixed[h * 8 : (h + 1) * 8]
            packed = jnp.where(lanes == h, lse[h * 8 : (h + 1) * 8], packed)
        lse_ref[pl.ds(row, 8), :] = packed
        return 0

    lax.fori_loop(0, reqs // per, group, 0)


def cached_attention(table, lengths, queries, pages):
    tokens, width = queries.shape
    heads = width // HD
    return pl.pallas_call(
        cached_kernel,
        in_specs=[SM, SM, VM, ANY],
        out_specs=(VM, VM),
        out_shape=(sds((heads, tokens, HD), jnp.float32), sds((tokens, HD), jnp.float32)),
        scratch_shapes=[
            pltpu.VMEM(pages.shape, pages.dtype),
            pltpu.VMEM(queries.shape, jnp.float32),
            pltpu.SemaphoreType.DMA((lengths.shape[0] * S // 8,)),
        ],
        compiler_params=params(24),
        name="cached_attention",
    )(table, lengths, queries, pages)


def attend_new(proj_k, proj_v, refs, new_k, new_v, low_ref, mixed_all):
    q_ref, cos_ref, sin_ref, acc_ref, lse_ref, slot_ref, a_refs = refs
    tokens = proj_k.shape[0]
    heads = q_ref.shape[1] // HD
    keys = (proj_k * cos_ref[...] + pltpu.roll(proj_k, HD // 2, 1) * sin_ref[...]).astype(
        jnp.bfloat16
    )
    values = proj_v.astype(jnp.bfloat16)
    new_k[...] = keys
    new_v[...] = values
    rows = lax.broadcasted_iota(jnp.int32, (tokens, tokens), 0)
    cols = lax.broadcasted_iota(jnp.int32, (tokens, tokens), 1)
    allowed = (rows // S == cols // S) & (cols <= rows)
    for h in range(heads):
        span = slice(h * HD, (h + 1) * HD)
        scores = lax.dot_general(q_ref[:, span], keys, NT, preferred_element_type=jnp.float32)
        scores = jnp.where(allowed, scores * SCALE, BIG)
        lse = lse_ref[:, h : h + 1]
        top = jnp.maximum(jnp.max(scores, axis=1, keepdims=True), lse)
        weights = jnp.exp(scores - top)
        old = jnp.exp(lse - top)
        total = jnp.sum(weights, axis=1, keepdims=True) + old
        mixed = jnp.dot(weights.astype(jnp.bfloat16), values, preferred_element_type=jnp.float32)
        mixed_all[:, span] = ((mixed + old * acc_ref[h]) / total).astype(jnp.bfloat16)
    slots = slot_ref[...]
    half = lax.broadcasted_iota(jnp.int32, (tokens, HD), 1) // R
    folded = jnp.zeros((tokens, HD), jnp.float32)
    base = 0
    for a_ref in a_refs:
        low = lax.dot_general(
            mixed_all[...], a_ref[...], NT, preferred_element_type=jnp.float32
        )
        for j in range(a_ref.shape[0] // HD):
            folded = folded + jnp.where(
                slots == base + 2 * j + half, low[:, j * HD : (j + 1) * HD], 0.0
            )
        base += a_ref.shape[0] // R
    folded = folded + pltpu.roll(folded, R, 1)
    low_ref[...] = jnp.where(
        half[: tokens // 2] == 0, folded[: tokens // 2], folded[tokens // 2 :]
    ).astype(jnp.bfloat16)


def first_kernel(n_tp, n_a, sec_ref, *refs):
    h_refs, (w_ref, gain_ref) = refs[:n_tp], refs[n_tp : n_tp + 2]
    shared = refs[n_tp + 2 : n_tp + 8]
    a_refs = refs[n_tp + 8 : n_tp + 8 + n_a]
    new_k, new_v, low_ref, mixed_all = refs[n_tp + 8 + n_a :]
    width = h_refs[0].shape[1]

    @pl.when(sec_ref[0] == 0)
    def _():
        tokens = h_refs[0].shape[0]
        proj = jnp.zeros((tokens, 2 * HD), jnp.float32)
        square = jnp.zeros((tokens, 1), jnp.float32)
        for s in range(n_tp):
            place = lax.rem(sec_ref[1] + n_tp - s, n_tp)
            row = pl.multiple_of(place * width, width)
            h = h_refs[s][...].astype(jnp.float32)
            square = square + jnp.sum(h * h, axis=1, keepdims=True)
            x = (h * gain_ref[pl.ds(place, 1), :]).astype(jnp.bfloat16)
            proj = proj + jnp.dot(
                x, w_ref[pl.ds(row, width), :], preferred_element_type=jnp.float32
            )
        proj = proj * lax.rsqrt(square / (n_tp * width) + EPS)
        attend_new(
            proj[:, :HD], proj[:, HD:], (*shared, a_refs), new_k, new_v, low_ref, mixed_all
        )

    @pl.when(sec_ref[0] != 0)
    def _():
        new_k[...] = jnp.zeros_like(new_k)
        new_v[...] = jnp.zeros_like(new_v)


def later_kernel(section, n_tp, n_a, total_width, sec_ref, *refs):
    m_refs = refs[:n_tp]
    shared = refs[n_tp : n_tp + 6]
    a_refs = refs[n_tp + 6 : n_tp + 6 + n_a]
    prev_k, prev_v, new_k, new_v, low_ref, mixed_all = refs[n_tp + 6 + n_a :]

    @pl.when(sec_ref[0] == section)
    def _():
        tokens = prev_k.shape[0]
        proj = jnp.zeros((tokens, 2 * HD), jnp.float32)
        square = jnp.zeros((1, HD), jnp.float32)
        for m_ref in m_refs:
            proj = proj + m_ref[:tokens, :].astype(jnp.float32)
            tail = m_ref[tokens : tokens + 16, :HD].astype(jnp.float32)
            square = square + jnp.sum(tail, axis=0, keepdims=True) * 0.125
        inv = lax.rsqrt(square / total_width + EPS)
        inv = jnp.transpose(jnp.broadcast_to(inv, (tokens, HD)))
        attend_new(
            proj[:, :HD] * inv,
            proj[:, HD:] * inv,
            (*shared, a_refs),
            new_k,
            new_v,
            low_ref,
            mixed_all,
        )

    @pl.when(sec_ref[0] != section)
    def _():
        new_k[...] = prev_k[...]
        new_v[...] = prev_v[...]


def attend_call(kernel, operands, tokens, q_width, name):
    return pl.pallas_call(
        kernel,
        in_specs=[SM] + [VM] * (len(operands) - 1),
        out_specs=(VM, VM, VM),
        out_shape=(
            sds((tokens, HD), jnp.bfloat16),
            sds((tokens, HD), jnp.bfloat16),
            sds((tokens // 2, HD), jnp.bfloat16),
        ),
        scratch_shapes=[pltpu.VMEM((tokens, q_width), jnp.bfloat16)],
        compiler_params=params(32),
        name=name,
    )(*operands)


def unfold_low(packed, slots, base, rows):
    count = packed.shape[0]
    half = lax.broadcasted_iota(jnp.int32, (count, HD), 1) // R
    turned = pltpu.roll(packed, R, 1)
    low = jnp.concatenate(
        [jnp.where(half == 0, packed, turned), jnp.where(half == 1, packed, turned)], axis=0
    )
    half = lax.broadcasted_iota(jnp.int32, (2 * count, HD), 1) // R
    return jnp.concatenate(
        [
            jnp.where(slots == base + 2 * j + half, low, 0.0).astype(jnp.bfloat16)
            for j in range(rows // HD)
        ],
        axis=1,
    )


def add_delta(low, slots, b_refs, h_ref, span):
    delta = None
    base = 0
    for b_ref, spread in zip(b_refs, low):
        part = jnp.dot(spread, b_ref[:, span], preferred_element_type=jnp.float32)
        delta = part if delta is None else delta + part
    delta = delta.astype(jnp.bfloat16).astype(jnp.float32)
    return (h_ref[:, span].astype(jnp.float32) + delta).astype(jnp.bfloat16)


def spreads(packed, slots, b_refs):
    out = []
    base = 0
    for b_ref in b_refs:
        out.append(unfold_low(packed, slots, base, b_ref.shape[0]))
        base += b_ref.shape[0] // R
    return out


def slice_kernel(section, n_tp, n_b, sec_ref, *refs):
    low_refs = refs[:n_tp]
    slot_ref, h_ref, gain_ref, w_ref = refs[n_tp : n_tp + 4]
    b_refs = refs[n_tp + 4 : n_tp + 4 + n_b]
    rest = refs[n_tp + 4 + n_b :]
    mine, other = rest[: n_tp - 1], rest[n_tp - 1 : 2 * n_tp - 2]
    h_out, low_out = rest[2 * n_tp - 2 : 2 * n_tp]
    m_refs = rest[2 * n_tp : 3 * n_tp]
    x_all = rest[3 * n_tp]
    tokens, width = h_ref.shape
    part = width // 4
    split = width // 2

    @pl.when(sec_ref[0] == section)
    def _():
        packed = low_refs[0][...].astype(jnp.float32)
        for low_ref in low_refs[1:]:
            packed = packed + low_ref[...].astype(jnp.float32)
        rounded = packed.astype(jnp.bfloat16)
        low_out[...] = rounded
        slots = slot_ref[...]
        low = spreads(rounded.astype(jnp.float32), slots, b_refs)
        square = jnp.zeros((tokens, 1), jnp.float32)
        for c in range(4):
            span = slice(c * part, (c + 1) * part)
            h = add_delta(low, slots, b_refs, h_ref, span)
            h_out[:, span] = h
            h = h.astype(jnp.float32)
            square = square + jnp.sum(h * h, axis=1, keepdims=True)
            x_all[:, span] = (h * gain_ref[:, span]).astype(jnp.bfloat16)
        square = jnp.transpose(jnp.broadcast_to(square, (tokens, HD)))[:16]
        high = square.astype(jnp.bfloat16).astype(jnp.float32)
        upper = lax.broadcasted_iota(jnp.int32, (16, HD), 0) < 8
        tail = jnp.where(upper, high, square - high).astype(jnp.bfloat16)
        row = pl.multiple_of(sec_ref[1] * width, width)
        here = pl.multiple_of(sec_ref[2] * split, split)
        there = pl.multiple_of((1 - sec_ref[2]) * split, split)
        for s in range(n_tp):
            if s == 0:
                proj = jnp.dot(
                    x_all[...], w_ref[pl.ds(row, width), :], preferred_element_type=jnp.float32
                )
            else:
                proj = jnp.dot(
                    x_all[:, pl.ds(here, split)],
                    mine[s - 1][...],
                    preferred_element_type=jnp.float32,
                ) + jnp.dot(
                    x_all[:, pl.ds(there, split)],
                    other[s - 1][...],
                    preferred_element_type=jnp.float32,
                )
            m_refs[s][:tokens, :] = proj.astype(jnp.bfloat16)
            m_refs[s][tokens:, :HD] = tail
            m_refs[s][tokens:, HD:] = jnp.zeros_like(tail)


def section_slice(section, n_tp, sec, lows, slots, h_prev, gain, weights, b_blocks, mine, other):
    tokens, width = h_prev.shape
    operands = [sec, *lows, slots, h_prev, gain, weights, *b_blocks, *mine, *other]
    return pl.pallas_call(
        functools.partial(slice_kernel, section, n_tp, len(b_blocks)),
        in_specs=[SM] + [VM] * (len(operands) - 1),
        out_specs=(VM,) * (2 + n_tp),
        out_shape=(
            sds((tokens, width), jnp.bfloat16),
            sds((tokens // 2, HD), jnp.bfloat16),
            *[sds((tokens + 16, 2 * HD), jnp.bfloat16)] * n_tp,
        ),
        scratch_shapes=[pltpu.VMEM((tokens, width), jnp.bfloat16)],
        compiler_params=params(48),
        name="section_slice_%d" % section,
    )(*operands)


def result_kernel(n_sec, n_tp, n_b, sec_ref, back_ref, *refs):
    low_refs = refs[:n_tp]
    slot_ref = refs[n_tp]
    h_refs = refs[n_tp + 1 : n_tp + 1 + n_sec]
    b_refs = refs[n_tp + 1 + n_sec : n_tp + 1 + n_sec + n_b]
    out_ref, h_buf, sem = refs[n_tp + 1 + n_sec + n_b :]
    for l in range(n_sec):

        @pl.when(sec_ref[0] == l)
        def _(l=l):
            copy = pltpu.make_async_copy(h_refs[l], h_buf, sem)
            copy.start()
            copy.wait()

    packed = low_refs[0][...].astype(jnp.float32)
    for low_ref in low_refs[1:]:
        packed = packed + low_ref[...].astype(jnp.float32)
    packed = jnp.where(sec_ref[0] == n_sec - 1, packed, back_ref[...].astype(jnp.float32))
    rounded = packed.astype(jnp.bfloat16).astype(jnp.float32)
    slots = slot_ref[...]
    low = spreads(rounded, slots, b_refs)
    part = h_buf.shape[1] // 4
    for c in range(4):
        span = slice(c * part, (c + 1) * part)
        out_ref[:, span] = add_delta(low, slots, b_refs, h_buf, span)


def section_result(n_sec, n_tp, sec, back, lows, slots, hs, b_blocks):
    tokens, width = hs[0].shape
    return pl.pallas_call(
        functools.partial(result_kernel, n_sec, n_tp, len(b_blocks)),
        in_specs=[SM] + [VM] * (2 + n_tp) + [ANY] * n_sec + [VM] * len(b_blocks),
        out_specs=VM,
        out_shape=sds((tokens, width), jnp.bfloat16),
        scratch_shapes=[
            pltpu.VMEM((tokens, width), jnp.bfloat16),
            pltpu.SemaphoreType.DMA,
        ],
        compiler_params=params(32),
        name="section_result",
    )(sec, back, *lows, slots, *hs, *b_blocks)


def leaving_kernel(src_ref, keep_ref, page_ref, at_ref, k_ref, v_ref, pages_ref, out_ref, sem):
    count = out_ref.shape[0]
    tokens = k_ref.shape[0]

    def start(i, _):
        pltpu.make_async_copy(pages_ref.at[src_ref[i]], out_ref.at[i], sem).start()
        return 0

    lax.fori_loop(0, count, start, 0)
    pltpu.make_async_copy(out_ref, out_ref, sem).wait()
    rows = lax.broadcasted_iota(jnp.int32, (PAGE, tokens), 0)
    spot = jnp.where(at_ref[...] == rows, page_ref[...], -1)

    def insert(i, _):
        hit = jnp.where(spot == src_ref[i], 1.0, 0.0)
        fresh = jnp.sum(hit, axis=1, keepdims=True) > 0.0
        hit = hit.astype(jnp.bfloat16)
        keep = keep_ref[i] > 0
        for part, new in enumerate((k_ref, v_ref)):
            value = jnp.dot(hit, new[...], preferred_element_type=jnp.float32)
            old = out_ref[i, part].astype(jnp.float32)
            value = jnp.where(keep, jnp.where(fresh, value, old), 0.0)
            out_ref[i, part] = value.astype(jnp.bfloat16)
        return 0

    lax.fori_loop(0, count, insert, 0)


def leaving_pages(src, keep, page_of, at, new_k, new_v, pages):
    count = src.shape[0]
    return pl.pallas_call(
        leaving_kernel,
        in_specs=[SM, SM, VM, VM, VM, VM, ANY],
        out_specs=VM,
        out_shape=sds((count, *pages.shape[1:]), jnp.bfloat16),
        scratch_shapes=[pltpu.SemaphoreType.DMA],
        compiler_params=params(16),
        name="leaving_pages",
    )(src, keep, page_of, at, new_k, new_v, pages)


def turn_tables(positions):
    half = HD // 2
    freq = jnp.exp(-math.log(500000.0) * (2.0 * jnp.arange(half, dtype=jnp.float32) / HD))
    angles = positions.astype(jnp.float32)[:, None] * freq
    cos, sin = jnp.cos(angles), jnp.sin(angles)
    return jnp.concatenate([cos, cos], axis=1), jnp.concatenate([-sin, sin], axis=1)


def body(
    hidden,
    queries,
    norm_gain,
    kv_weight,
    adapter_in,
    adapter_out,
    kv_pages,
    adapter_ids,
    owner_rows,
    page_table,
    lengths,
    moves,
):
    n_sec, n_req, n_tp = (lax.axis_size(a) for a in ("pipe", "req", "tp"))
    section, my_req, my_tp = (lax.axis_index(a) for a in ("pipe", "req", "tp"))
    tokens, width = hidden.shape
    depth = width * n_tp
    adapters = adapter_in.shape[1]
    q_width = queries.shape[2]
    half = width // 2

    def across(x, shift, sections):
        pairs = [
            (l * n_tp + t, l * n_tp + (t + shift) % n_tp) for l in sections for t in range(n_tp)
        ]
        return lax.ppermute(x, ("pipe", "tp"), pairs)

    def onward(x, shift, l):
        pairs = [((l - 1) * n_tp + t, l * n_tp + (t + shift) % n_tp) for t in range(n_tp)]
        return lax.ppermute(x, ("pipe", "tp"), pairs)

    def partner(x):
        return lax.ppermute(x, "req", [(i, i ^ 1) for i in range(n_req)])

    later = list(range(1, n_sec))
    sec = jnp.stack([section, my_tp, my_req % 2]).astype(jnp.int32)
    a_own = adapter_in[0].reshape(adapters * R, q_width)
    b_own = adapter_out[0].reshape(adapters * R, width)
    store = owner_rows[adapter_ids]
    if n_req == 2:
        slot = jnp.where(store // adapters == my_req, 0, adapters) + store % adapters
        gather_a = lambda x: [x, partner(x)]
    else:
        slot = store
        gather_a = lambda x: [lax.all_gather(x, "req", axis=0, tiled=True)]
    slots = jnp.repeat(slot, S)[:, None]
    positions = (lengths[:, None] + jnp.arange(S, dtype=jnp.int32)[None, :]).reshape(tokens)
    cos, sin = turn_tables(positions)
    page_of = jnp.take_along_axis(
        page_table, positions.reshape(-1, S) // PAGE, axis=1
    ).reshape(1, tokens)
    at = (positions % PAGE).reshape(1, tokens)
    gains = norm_gain[0].astype(jnp.float32).reshape(n_tp, width)
    gain = lax.dynamic_slice_in_dim(gains, my_tp, 1, axis=0)

    rows_in = [hidden] + [across(hidden, s, [0]) for s in range(1, n_tp)]
    a_blocks = gather_a(a_own)
    b_blocks = gather_a(b_own)
    weights = split_parts(kv_weight[0].reshape(2 * depth, HD))
    acc, lse = cached_attention(page_table.reshape(-1), lengths, queries[0], kv_pages[0])

    mine, other = [], []
    for s in range(1, n_tp):
        row = ((my_tp + s) % n_tp) * width + (my_req % 2) * half
        piece = lax.dynamic_slice_in_dim(weights, row, half, axis=0)
        mine.append(across(piece, s, later))
        other.append(partner(mine[-1]))
    before = [
        lax.ppermute(b, "pipe", [(l, l + 1) for l in range(n_sec - 1)]) for b in b_blocks
    ]

    shared = [queries[0], cos, sin, acc, lse, slots, *a_blocks]
    n_a = len(a_blocks)
    new_k, new_v, low = attend_call(
        functools.partial(first_kernel, n_tp, n_a),
        [sec, *rows_in, weights, gains, *shared],
        tokens,
        q_width,
        "first_section",
    )
    hs = [hidden]
    h_prev = hidden
    sums = []
    for l in later:
        lows = [onward(low, s, l) for s in range(n_tp)]
        h_new, low_sum, *parts = section_slice(
            l, n_tp, sec, lows, slots, h_prev, gain, weights, before, mine, other
        )
        hs.append(h_new)
        sums.append(low_sum)
        parts = [parts[0]] + [across(parts[s], -s, [l]) for s in range(1, n_tp)]
        if l + 1 < n_sec:
            h_prev = lax.ppermute(h_new, "pipe", [(l, l + 1)])
        new_k, new_v, low = attend_call(
            functools.partial(later_kernel, l, n_tp, n_a, depth),
            [sec, *parts, *shared, new_k, new_v],
            tokens,
            q_width,
            "section_%d" % l,
        )
    lows = [low] + [across(low, s, [n_sec - 1]) for s in range(1, n_tp)]
    back = sums[0]
    for l in later[1:]:
        back = jnp.where(section == l, sums[l - 1], back)
    back = lax.ppermute(back, "pipe", [(l, l - 1) for l in later])
    section_out = section_result(n_sec, n_tp, sec, back, lows, slots, hs, b_blocks)

    count = moves.shape[0]
    if n_req == 2:
        match = moves[:, 2][None, :] == jnp.arange(count, dtype=jnp.int32)[:, None]
        src = jnp.sum(jnp.where(match, moves[:, 1][None, :], 0), axis=1)
        keep = jnp.sum(match.astype(jnp.int32), axis=1)
        leaving = leaving_pages(src, keep, page_of, at, new_k, new_v, kv_pages[0])
        arrived = partner(leaving)
    else:
        keep = jnp.ones((count,), jnp.int32)
        leaving = leaving_pages(moves[:, 1], keep, page_of, at, new_k, new_v, kv_pages[0])
        free_slots = (n_req - 1) * ((count + n_req - 2) // (n_req - 1))
        received, dest_in, spots_in = (
            lax.all_gather(x, "req", axis=0, tiled=True)
            for x in (leaving, moves[:, 0], moves[:, 2])
        )
        target = jnp.where(dest_in == my_req, spots_in, free_slots)
        empty = jnp.zeros((free_slots, *leaving.shape[1:]), jnp.bfloat16)
        arrived = empty.at[target].set(received, mode="drop")
    new_kv = jnp.stack([new_k, new_v], axis=1)
    return (section_out[None], new_kv[None], arrived[None])


def solution(mesh):
    in_specs = (
        P("req", "tp"),
        P("pipe", "req", "tp"),
        P("pipe", None),
        P("pipe", None, None, "tp"),
        P("pipe", "req", None, "tp"),
        P("pipe", "req", None, "tp"),
        P("pipe", "req", None, None, "tp"),
        P("req"),
        P(),
        P("req", None),
        P("req"),
        P("req", None),
    )
    out_specs = (
        P("pipe", "req", "tp"),
        P("pipe", "req", None, "tp"),
        P("pipe", "req", None, None, "tp"),
    )
    return jax.shard_map(body, mesh=mesh, in_specs=in_specs, out_specs=out_specs, check_vma=False)
```

```python
import functools
import math

import jax
import jax.numpy as jnp
from jax import lax
from jax.experimental import pallas as pl
from jax.experimental.pallas import tpu as pltpu
from jax.sharding import PartitionSpec as P

HD = 128
R = 64
S = 4
PAGE = 64
MAXP = 4
EPS = 1e-05
BIG = -1e30
VMEM_MIB = 32
SCALE = HD ** (-0.5)
VM = pl.BlockSpec(memory_space=pltpu.VMEM)
SM = pl.BlockSpec(memory_space=pltpu.SMEM)
ANY = pl.BlockSpec(memory_space=pltpu.HBM)
NT = (((1,), (1,)), ((), ()))


def vmem(mib=VMEM_MIB):
    return pltpu.CompilerParams(vmem_limit_bytes=mib << 20)


def kept(shape, dtype):
    return pltpu.VMEM(shape, dtype)


def in_hbm(x):
    return pltpu.with_memory_space_constraint(x, pltpu.HBM)


def cost(micros):
    return pl.CostEstimate(flops=0, bytes_accessed=int(micros * 3_000_000), transcendentals=0)


def sds(shape, dtype):
    return jax.ShapeDtypeStruct(shape, dtype)


def halves_of(rows):
    return rows // 2


def split_kernel(chunks, section_of, sec_ref, *refs):
    raw_refs, (out_ref, buf, wide, sems) = refs[:-4], refs[-4:]
    rows = buf.shape[1] // 2

    @pl.when(section_of(sec_ref[0]))
    def _():
        loads = []
        for index, (source, start, _) in enumerate(chunks):
            first = pl.multiple_of(start(sec_ref) * 2 * rows, 2 * rows)
            loads.append(
                pltpu.make_async_copy(
                    raw_refs[source].at[pl.ds(first, 2 * rows)], buf.at[index], sems.at[index]
                )
            )
            loads[-1].start()
        for index, (_, _, to) in enumerate(chunks):
            loads[index].wait()
            wide[...] = buf[index].astype(jnp.float32)
            out = pl.ds(pl.multiple_of(to(sec_ref) * rows, rows), rows)
            out_ref[out, :HD] = wide[pl.ds(0, rows, stride=2), :].astype(jnp.bfloat16)
            out_ref[out, HD:] = wide[pl.ds(1, rows, stride=2), :].astype(jnp.bfloat16)


def split_parts(sec, raws, chunks, section_of, rows, name):
    return pl.pallas_call(
        functools.partial(split_kernel, chunks, section_of),
        in_specs=[SM] + [ANY] * len(raws),
        out_specs=VM,
        out_shape=kept((rows * len(chunks), 2 * HD), jnp.bfloat16),
        scratch_shapes=[
            pltpu.VMEM((len(chunks), 2 * rows, HD), jnp.bfloat16),
            pltpu.VMEM((2 * rows, HD), jnp.float32),
            pltpu.SemaphoreType.DMA((len(chunks),)),
        ],
        compiler_params=vmem(),
        cost_estimate=cost(5),
        name=name,
    )(sec, *[in_hbm(x) for x in raws])


def parcel_kernel(n_tp, sec_ref, h_ref, raw_ref, *refs):
    out_refs, sems = refs[:-1], refs[-1]
    rows = out_refs[0].shape[0]
    width = h_ref.shape[1]

    @pl.when(sec_ref[0] == 0)
    def _():
        for out in out_refs:
            for c in range(width // HD):
                out[c * HD : (c + 1) * HD, :] = h_ref[:, c * HD : (c + 1) * HD]

    @pl.when(sec_ref[0] != 0)
    def _():
        loads = []
        for s in range(1, n_tp):
            place = lax.rem(sec_ref[1] + s, n_tp) * 2 + sec_ref[2]
            first = pl.multiple_of(place * rows, rows)
            loads.append(
                pltpu.make_async_copy(
                    raw_ref.at[pl.ds(first, rows)], out_refs[s - 1], sems.at[s - 1]
                )
            )
            loads[-1].start()
        for load in loads:
            load.wait()


def parcels(sec, hidden, raw, n_tp):
    tokens, width = hidden.shape
    rows = raw.shape[0] // (2 * n_tp)
    assert tokens == HD and rows * HD == tokens * width
    return pl.pallas_call(
        functools.partial(parcel_kernel, n_tp),
        in_specs=[SM, VM, ANY],
        out_specs=(VM,) * (n_tp - 1),
        out_shape=(sds((rows, HD), jnp.bfloat16),) * (n_tp - 1),
        scratch_shapes=[pltpu.SemaphoreType.DMA((n_tp - 1,))],
        compiler_params=vmem(),
        cost_estimate=cost(2),
        name="parcels",
    )(sec, hidden, in_hbm(raw))


def local_kernel(
    paired,
    adapters,
    sec_ref,
    table_ref,
    len_ref,
    ids_ref,
    rows_ref,
    move_ref,
    q_ref,
    pages_ref,
    acc_ref,
    lse_ref,
    slot_ref,
    cos_ref,
    sin_ref,
    leave_ref,
    spot_ref,
    buf,
    place,
    sems,
    leave_sem,
):
    heads, tokens, _ = acc_ref.shape
    reqs = tokens // S
    moves = leave_ref.shape[0]
    per = 16 // S
    ctx = MAXP * PAGE
    pages = per * MAXP

    def start(i, _):
        page = table_ref[i]
        place[page] = i
        pltpu.make_async_copy(pages_ref.at[page], buf.at[i], sems.at[i // pages]).start()
        return 0

    lax.fori_loop(0, reqs * MAXP, start, 0, unroll=8)
    lanes = lax.broadcasted_iota(jnp.int32, (1, tokens), 1)

    def leave(i, _):
        page = move_ref[3 * i + 1]
        to = move_ref[3 * i + 2] if paired else i
        pltpu.make_async_copy(pages_ref.at[page], leave_ref.at[to], leave_sem).start()
        index = place[page]
        req = index // MAXP
        position = len_ref[req] + lanes % S
        hit = (lanes // S == req) & (position // PAGE == index % MAXP)
        spot_ref[pl.ds(to, 1), :] = jnp.where(hit, position % PAGE, -1)
        return 0

    lax.fori_loop(0, moves, leave, 0)

    eight = lax.broadcasted_iota(jnp.int32, (8, HD), 0)
    freq = jnp.exp(
        (-math.log(500000.0) * 2.0 / HD)
        * (lax.broadcasted_iota(jnp.int32, (8, HD), 1) % (HD // 2)).astype(jnp.float32)
    )
    sign = jnp.where(lax.broadcasted_iota(jnp.int32, (8, HD), 1) < HD // 2, -1.0, 1.0)
    for i in range(tokens // 8):
        slot, length = [], []
        for r in (2 * i, 2 * i + 1):
            row = rows_ref[ids_ref[r]]
            if paired:
                away = jnp.where(row // adapters == sec_ref[3], 0, adapters)
                row = row % adapters + away
            slot.append(row)
            length.append(len_ref[r])
        span = slice(8 * i, 8 * i + 8)
        first = eight < S
        slot_ref[span, :] = jnp.where(first, slot[0], slot[1])
        position = jnp.where(first, length[0], length[1]) + eight % S
        angle = position.astype(jnp.float32) * freq
        cos_ref[span, :] = jnp.cos(angle)
        sin_ref[span, :] = jnp.sin(angle) * sign

    lane = lax.broadcasted_iota(jnp.int32, (ctx, HD), 1)
    mine = (lane % 16) // S
    lane16 = lax.broadcasted_iota(jnp.int32, (16, HD), 1)
    key_at = lax.broadcasted_iota(jnp.int32, (ctx, HD), 0)
    row_of = (lax.broadcasted_iota(jnp.int32, (HD, HD), 0) % 16) // S

    def group(g, _):
        first = pl.multiple_of(g * pages, pages)
        block = buf.at[pl.ds(first, pages)]
        pltpu.make_async_copy(block, block, sems.at[g]).wait()
        row = pl.multiple_of(g * 16, 16)
        q = jnp.concatenate(
            [q_ref[pl.ds(row, 16), h * HD : (h + 1) * HD] for h in range(heads)], axis=0
        )
        scores = None
        limit = None
        for r in range(per):
            keys = buf[pl.ds(first + r * MAXP, MAXP), 0].reshape(ctx, HD)
            part = lax.dot_general(keys, q, NT, preferred_element_type=jnp.float32)
            length = len_ref[g * per + r]
            scores = part if r == 0 else jnp.where(mine == r, part, scores)
            limit = length if r == 0 else jnp.where(mine[:1] == r, length, limit)
        scores = jnp.where(key_at < limit, scores * SCALE, BIG)
        top = jnp.max(scores, axis=0, keepdims=True)
        weights = jnp.exp(scores - top)
        total = jnp.sum(weights, axis=0, keepdims=True)
        column = jnp.transpose(jnp.broadcast_to(top + jnp.log(total), (HD, HD)))
        packed = column[:16]
        for h in range(1, heads):
            packed = jnp.where(lane16 == h, column[h * 16 : (h + 1) * 16], packed)
        lse_ref[pl.ds(row, 16), :] = packed
        weights = jnp.transpose(weights * (1.0 / total)).astype(jnp.bfloat16)
        mixed = None
        for r in range(per):
            values = buf[pl.ds(first + r * MAXP, MAXP), 1].reshape(ctx, HD)
            part = jnp.dot(weights, values, preferred_element_type=jnp.float32)
            mixed = part if r == 0 else jnp.where(row_of == r, part, mixed)
        for h in range(heads):
            acc_ref[h, pl.ds(row, 16), :] = mixed[h * 16 : (h + 1) * 16]
        return 0

    lax.fori_loop(0, reqs // per, group, 0, unroll=2)
    pltpu.make_async_copy(leave_ref, leave_ref, leave_sem).wait()


def local_work(paired, adapters, sec, table, lengths, ids, rows, moves, queries, pages):
    tokens, width = queries.shape
    heads = width // HD
    count = moves.shape[0] // 3
    groups = tokens // 16
    square = (tokens, HD)
    return pl.pallas_call(
        functools.partial(local_kernel, paired, adapters),
        in_specs=[SM] * 6 + [VM, ANY],
        out_specs=(VM,) * 7,
        out_shape=(
            kept((heads, tokens, HD), jnp.float32),
            kept(square, jnp.float32),
            kept(square, jnp.int32),
            kept(square, jnp.float32),
            kept(square, jnp.float32),
            sds((count, *pages.shape[1:]), jnp.bfloat16),
            sds((count, tokens), jnp.int32),
        ),
        scratch_shapes=[
            pltpu.VMEM(pages.shape, pages.dtype),
            pltpu.SMEM((pages.shape[0],), jnp.int32),
            pltpu.SemaphoreType.DMA((groups,)),
            pltpu.SemaphoreType.DMA,
        ],
        compiler_params=vmem(),
        cost_estimate=cost(10),
        name="local_work",
    )(sec, table, lengths, ids, rows, moves, queries, in_hbm(pages))


def attend_new(proj_k, proj_v, refs, fresh_ref, low_ref, mixed_all, loads):
    q_ref, cos_ref, sin_ref, acc_ref, lse_ref, slot_ref, a_refs = refs
    tokens = proj_k.shape[0]
    heads = q_ref.shape[1] // HD
    keys = (proj_k * cos_ref[...] + pltpu.roll(proj_k, HD // 2, 1) * sin_ref[...]).astype(
        jnp.bfloat16
    )
    values = proj_v.astype(jnp.bfloat16)
    fresh_ref[:, :HD] = keys
    fresh_ref[:, HD:] = values
    rows = lax.broadcasted_iota(jnp.int32, (tokens, tokens), 0)
    cols = lax.broadcasted_iota(jnp.int32, (tokens, tokens), 1)
    allowed = (rows // S == cols // S) & (cols <= rows)
    for h in range(heads):
        span = slice(h * HD, (h + 1) * HD)
        scores = lax.dot_general(q_ref[:, span], keys, NT, preferred_element_type=jnp.float32)
        scores = jnp.where(allowed, scores * SCALE, BIG)
        lse = lse_ref[:, h : h + 1]
        top = jnp.maximum(jnp.max(scores, axis=1, keepdims=True), lse)
        weights = jnp.exp(scores - top)
        old = jnp.exp(lse - top)
        total = jnp.sum(weights, axis=1, keepdims=True) + old
        mixed = jnp.dot(weights.astype(jnp.bfloat16), values, preferred_element_type=jnp.float32)
        mixed_all[:, span] = ((mixed + old * acc_ref[h]) / total).astype(jnp.bfloat16)
    slots = slot_ref[...]
    half = lax.broadcasted_iota(jnp.int32, (tokens, HD), 1) // R
    folded = jnp.zeros((tokens, HD), jnp.float32)
    base = 0
    for a_ref, load in zip(a_refs, loads):
        load.wait()
        low = lax.dot_general(
            mixed_all[...], a_ref[...], NT, preferred_element_type=jnp.float32
        )
        for j in range(a_ref.shape[0] // HD):
            folded = folded + jnp.where(
                slots == base + 2 * j + half, low[:, j * HD : (j + 1) * HD], 0.0
            )
        base += a_ref.shape[0] // R
    folded = folded + pltpu.roll(folded, R, 1)
    low_ref[...] = jnp.where(
        half[: tokens // 2] == 0, folded[: tokens // 2], folded[tokens // 2 :]
    ).astype(jnp.bfloat16)


def start_loads(sources, targets, sems):
    loads = [
        pltpu.make_async_copy(source, target, sems.at[i])
        for i, (source, target) in enumerate(zip(sources, targets))
    ]
    for load in loads:
        load.start()
    return loads


def first_kernel(n_tp, n_a, sec_ref, *refs):
    h_refs, (w_ref, gain_ref) = refs[:n_tp], refs[n_tp : n_tp + 2]
    shared = refs[n_tp + 2 : n_tp + 8]
    a_refs = refs[n_tp + 8 : n_tp + 8 + n_a]
    fresh_ref, low_ref, mixed_all, *a_bufs, sems = refs[n_tp + 8 + n_a :]
    width = h_refs[0].shape[1]

    @pl.when(sec_ref[0] == 0)
    def _():
        loads = start_loads(a_refs, a_bufs, sems)
        tokens = h_refs[0].shape[0]
        proj = jnp.zeros((tokens, 2 * HD), jnp.float32)
        square = jnp.zeros((tokens, 1), jnp.float32)
        for s in range(n_tp):
            place = lax.rem(sec_ref[1] + n_tp - s, n_tp)
            lane = pl.multiple_of(place * width, width)
            row = pl.multiple_of(place * width, width)
            if s == 0:
                h = h_refs[s][...]
            else:
                h = jnp.concatenate(
                    [h_refs[s][c * HD : (c + 1) * HD, :] for c in range(width // HD)], axis=1
                )
            h = h.astype(jnp.float32)
            square = square + jnp.sum(h * h, axis=1, keepdims=True)
            x = (h * gain_ref[:, pl.ds(lane, width)].astype(jnp.float32)).astype(jnp.bfloat16)
            proj = proj + jnp.dot(
                x, w_ref[pl.ds(row, width), :], preferred_element_type=jnp.float32
            )
        proj = proj * lax.rsqrt(square / (n_tp * width) + EPS)
        attend_new(
            proj[:, :HD], proj[:, HD:], (*shared, a_bufs), fresh_ref, low_ref, mixed_all, loads
        )


def later_kernel(section, n_tp, n_a, total_width, sec_ref, *refs):
    m_refs = refs[:n_tp]
    shared = refs[n_tp : n_tp + 6]
    a_refs = refs[n_tp + 6 : n_tp + 6 + n_a]
    fresh_ref, low_ref, mixed_all, *a_bufs, sems = refs[n_tp + 6 + n_a :]

    @pl.when(sec_ref[0] == section)
    def _():
        loads = start_loads(a_refs, a_bufs, sems)
        tokens = fresh_ref.shape[0]
        proj = jnp.zeros((tokens, 2 * HD), jnp.float32)
        square = jnp.zeros((1, HD), jnp.float32)
        for m_ref in m_refs:
            proj = proj + m_ref[:tokens, :].astype(jnp.float32)
            tail = m_ref[tokens : tokens + 16, :HD].astype(jnp.float32)
            square = square + jnp.sum(tail, axis=0, keepdims=True) * 0.125
        inv = lax.rsqrt(square / total_width + EPS)
        inv = jnp.transpose(jnp.broadcast_to(inv, (tokens, HD)))
        attend_new(
            proj[:, :HD] * inv,
            proj[:, HD:] * inv,
            (*shared, a_bufs),
            fresh_ref,
            low_ref,
            mixed_all,
            loads,
        )


def attend_call(kernel, operands, a_blocks, tokens, q_width, name):
    return pl.pallas_call(
        kernel,
        in_specs=[SM] + [VM] * (len(operands) - 1) + [ANY] * len(a_blocks),
        out_specs=(VM, VM),
        out_shape=(
            sds((tokens, 2 * HD), jnp.bfloat16),
            sds((tokens // 2, HD), jnp.bfloat16),
        ),
        scratch_shapes=[
            pltpu.VMEM((tokens, q_width), jnp.bfloat16),
            *[pltpu.VMEM(a.shape, jnp.bfloat16) for a in a_blocks],
            pltpu.SemaphoreType.DMA((len(a_blocks),)),
        ],
        compiler_params=vmem(),
        cost_estimate=cost(5),
        name=name,
    )(*operands, *[in_hbm(a) for a in a_blocks])


def unfold_low(packed, slots, base, rows):
    count = packed.shape[0]
    half = lax.broadcasted_iota(jnp.int32, (count, HD), 1) // R
    turned = pltpu.roll(packed, R, 1)
    low = jnp.concatenate(
        [jnp.where(half == 0, packed, turned), jnp.where(half == 1, packed, turned)], axis=0
    )
    half = lax.broadcasted_iota(jnp.int32, (2 * count, HD), 1) // R
    return jnp.concatenate(
        [
            jnp.where(slots == base + 2 * j + half, low, 0.0).astype(jnp.bfloat16)
            for j in range(rows // HD)
        ],
        axis=1,
    )


def add_delta(low, b_refs, h, span):
    delta = None
    for b_ref, spread in zip(b_refs, low):
        part = jnp.dot(spread, b_ref[:, span], preferred_element_type=jnp.float32)
        delta = part if delta is None else delta + part
    delta = delta.astype(jnp.bfloat16).astype(jnp.float32)
    return (h.astype(jnp.float32) + delta).astype(jnp.bfloat16)


def spreads(packed, slots, b_refs):
    out = []
    base = 0
    for b_ref in b_refs:
        out.append(unfold_low(packed, slots, base, b_ref.shape[0]))
        base += b_ref.shape[0] // R
    return out


def slice_kernel(section, n_tp, n_b, sec_ref, *refs):
    low_refs = refs[:n_tp]
    slot_ref, gain_ref, w_ref, h_ref = refs[n_tp : n_tp + 4]
    b_refs = refs[n_tp + 4 : n_tp + 4 + n_b]
    rest = refs[n_tp + 4 + n_b :]
    h_out, m_refs = rest[0], rest[1 : 1 + n_tp]
    x_all, h_buf = rest[1 + n_tp : 3 + n_tp]
    b_bufs = rest[3 + n_tp : 3 + n_tp + n_b]
    sems = rest[3 + n_tp + n_b]
    tokens, width = h_buf.shape
    part = width // 4

    @pl.when(sec_ref[0] == section)
    def _():
        loads = [pltpu.make_async_copy(h_ref, h_buf, sems.at[0])]
        for i in range(n_b):
            loads.append(pltpu.make_async_copy(b_refs[i], b_bufs[i], sems.at[1 + i]))
        for load in loads:
            load.start()
        packed = low_refs[0][...].astype(jnp.float32)
        for low_ref in low_refs[1:]:
            packed = packed + low_ref[...].astype(jnp.float32)
        rounded = packed.astype(jnp.bfloat16)
        low = spreads(rounded.astype(jnp.float32), slot_ref[...], b_refs)
        for load in loads:
            load.wait()
        square = jnp.zeros((tokens, 1), jnp.float32)
        for c in range(4):
            span = slice(c * part, (c + 1) * part)
            h = add_delta(low, b_bufs, h_buf[:, span], span)
            h_buf[:, span] = h
            h = h.astype(jnp.float32)
            square = square + jnp.sum(h * h, axis=1, keepdims=True)
            lane = pl.multiple_of(sec_ref[1] * width + c * part, part)
            gain = gain_ref[:, pl.ds(lane, part)].astype(jnp.float32)
            x_all[:, span] = (h * gain).astype(jnp.bfloat16)
        store = pltpu.make_async_copy(h_buf, h_out, sems.at[0])
        store.start()
        square = jnp.transpose(jnp.broadcast_to(square, (tokens, HD)))[:16]
        high = square.astype(jnp.bfloat16).astype(jnp.float32)
        upper = lax.broadcasted_iota(jnp.int32, (16, HD), 0) < 8
        tail = jnp.where(upper, high, square - high).astype(jnp.bfloat16)
        for s in range(n_tp):
            rows = pl.ds(s * width, width)
            proj = jnp.dot(x_all[...], w_ref[rows, :], preferred_element_type=jnp.float32)
            m_refs[s][:tokens, :] = proj.astype(jnp.bfloat16)
            m_refs[s][tokens:, :HD] = tail
            m_refs[s][tokens:, HD:] = jnp.zeros_like(tail)
        store.wait()


def section_slice(section, n_tp, sec, lows, slots, gain, h_prev, weights, b_blocks):
    tokens, width = h_prev.shape
    operands = [sec, *lows, slots, gain, weights, *[in_hbm(x) for x in (h_prev, *b_blocks)]]
    return pl.pallas_call(
        functools.partial(slice_kernel, section, n_tp, len(b_blocks)),
        in_specs=[SM] + [VM] * (n_tp + 3) + [ANY] * (1 + len(b_blocks)),
        out_specs=(ANY,) + (VM,) * n_tp,
        out_shape=(
            sds((tokens, width), jnp.bfloat16),
            *[sds((tokens + 16, 2 * HD), jnp.bfloat16)] * n_tp,
        ),
        scratch_shapes=[
            pltpu.VMEM((tokens, width), jnp.bfloat16),
            pltpu.VMEM((tokens, width), jnp.bfloat16),
            *[pltpu.VMEM(b.shape, jnp.bfloat16) for b in b_blocks],
            pltpu.SemaphoreType.DMA((1 + len(b_blocks),)),
        ],
        compiler_params=vmem(),
        cost_estimate=cost(5),
        name="section_slice_%d" % section,
    )(*operands)


def result_kernel(last, n_tp, n_b, sec_ref, back_ref, *refs):
    low_refs = refs[:n_tp]
    slot_ref, h_ref = refs[n_tp : n_tp + 2]
    b_refs = refs[n_tp + 2 : n_tp + 2 + n_b]
    out_ref = refs[n_tp + 2 + n_b]

    @pl.when(sec_ref[0] != last)
    def _():
        out_ref[0] = back_ref[...]

    @pl.when(sec_ref[0] == last)
    def _():
        packed = low_refs[0][...].astype(jnp.float32)
        for low_ref in low_refs[1:]:
            packed = packed + low_ref[...].astype(jnp.float32)
        rounded = packed.astype(jnp.bfloat16).astype(jnp.float32)
        slots = slot_ref[...]
        low = spreads(rounded, slots, b_refs)
        part = h_ref.shape[1] // 4
        for c in range(4):
            span = slice(c * part, (c + 1) * part)
            out_ref[0, :, span] = add_delta(low, b_refs, h_ref[:, span], span)


def section_result(last, n_tp, sec, back, lows, slots, held, b_blocks):
    operands = [sec, back, *lows, slots, held, *b_blocks]
    return pl.pallas_call(
        functools.partial(result_kernel, last, n_tp, len(b_blocks)),
        in_specs=[SM] + [VM] * (len(operands) - 1),
        out_specs=VM,
        out_shape=sds((1, *held.shape), jnp.bfloat16),
        compiler_params=vmem(),
        cost_estimate=cost(3),
        name="section_result",
    )(*operands)


def insert_kernel(spot_ref, new_ref, old_ref, out_ref):
    count = old_ref.shape[0]
    tokens = new_ref.shape[0]
    rows = lax.broadcasted_iota(jnp.int32, (PAGE, tokens), 0)

    def insert(i, _):
        spot = spot_ref[pl.ds(i, 1), :]
        hit = jnp.where(spot == rows, 1.0, 0.0)
        fresh = jnp.sum(hit, axis=1, keepdims=True) > 0.0
        hit = hit.astype(jnp.bfloat16)
        values = jnp.dot(hit, new_ref[...], preferred_element_type=jnp.float32)
        for part in range(2):
            value = values[:, part * HD : (part + 1) * HD]
            old = old_ref[i, part].astype(jnp.float32)
            out_ref[0, i, part] = jnp.where(fresh, value, old).astype(jnp.bfloat16)
        return 0

    lax.fori_loop(0, count, insert, 0, unroll=4)


def insert_new(spots, fresh, old):
    return pl.pallas_call(
        insert_kernel,
        in_specs=[VM] * 3,
        out_specs=VM,
        out_shape=sds((1, *old.shape), jnp.bfloat16),
        compiler_params=vmem(),
        cost_estimate=cost(3),
        name="insert_new",
    )(spots, fresh, old)


def body(
    hidden,
    queries,
    norm_gain,
    kv_weight,
    adapter_in,
    adapter_out,
    kv_pages,
    adapter_ids,
    owner_rows,
    page_table,
    lengths,
    moves,
):
    n_sec, n_req, n_tp = (lax.axis_size(a) for a in ("pipe", "req", "tp"))
    section, my_req, my_tp = (lax.axis_index(a) for a in ("pipe", "req", "tp"))
    tokens, width = hidden.shape
    depth = width * n_tp
    adapters = adapter_in.shape[1]
    q_width = queries.shape[2]

    def around(x, shift):
        return lax.ppermute(x, "tp", [(t, (t + shift) % n_tp) for t in range(n_tp)])

    def onward(x, shift, step=1, sections=range(n_sec)):
        pairs = [
            (l * n_tp + t, (l + step) % n_sec * n_tp + (t + shift) % n_tp)
            for l in sections
            for t in range(n_tp)
        ]
        return lax.ppermute(x, ("pipe", "tp"), pairs)

    def partner(x, sections=range(n_sec), step=0):
        pairs = [
            (l * n_req + i, (l + step) % n_sec * n_req + (i ^ 1))
            for l in sections
            for i in range(n_req)
        ]
        return lax.ppermute(x, ("pipe", "req"), pairs)

    def gather(x):
        return [x, partner(x)] if paired else [lax.all_gather(x, "req", axis=0, tiled=True)]

    def after(x, *others):
        return lax.optimization_barrier((x, *others))[0]

    paired = n_req == 2
    later = list(range(1, n_sec))
    sec = jnp.stack([section, my_tp, my_req % 2, my_req]).astype(jnp.int32)

    a_own = adapter_in[0].reshape(adapters * R, q_width)
    b_own = adapter_out[0].reshape(adapters * R, width)
    raw = kv_weight[0].reshape(2 * depth, HD)
    half = width // 2
    final = n_sec - 1
    sent = parcels(sec, hidden, raw, n_tp)
    mine = [around(sent[s - 1], s) for s in range(1, n_tp)]
    a_blocks = gather(a_own)
    acc, lse, slots, cos, sin, leaving, spots = local_work(
        paired,
        adapters,
        sec,
        page_table.reshape(-1),
        lengths,
        adapter_ids,
        owner_rows,
        moves.reshape(-1),
        queries[0],
        kv_pages[0],
    )
    if paired:
        spots = partner(spots)
        ready = after(b_own, lse)
        own_before = onward(ready, 0)
        early = partner(ready, [0], 1)
    else:
        b_blocks = [lax.all_gather(b_own, "req", axis=0, tiled=True)]
        before = [onward(b_blocks[0], 0)]
    chunks = [(0, lambda sec, i=i: i, lambda sec, i=i: i) for i in range(2 * n_tp)]
    weights = split_parts(
        sec,
        [after(raw, lse, *a_blocks)],
        chunks,
        lambda section: section == 0,
        half,
        "split_first",
    )
    other = [partner(after(m, lse), later) for m in mine]

    shared = [queries[0], cos, sin, acc, lse, slots]
    n_a = len(a_blocks)
    fresh, low = attend_call(
        functools.partial(first_kernel, n_tp, n_a),
        [sec, hidden, *mine, weights, norm_gain, *shared],
        a_blocks,
        tokens,
        q_width,
        "first_section",
    )
    chunks = [(0, lambda sec, i=i: 2 * sec[1] + i, lambda sec, i=i: i) for i in range(2)]
    for s in range(1, n_tp):
        chunks.append((s, lambda sec: 0, lambda sec, s=s: 2 * s + sec[2]))
    for s in range(1, n_tp):
        chunks.append((n_tp - 1 + s, lambda sec: 0, lambda sec, s=s: 2 * s + 1 - sec[2]))
    own_rows = split_parts(
        sec,
        [after(raw, low), *mine, *other],
        chunks,
        lambda section: section > 0,
        half,
        "split_later",
    )
    h_prev = h_new = hidden
    hs, news = [hidden], [fresh]
    for l in later:
        lows = [onward(low, s, 1, [0] if l == 1 else range(n_sec)) for s in range(n_tp)]
        if l == 1 and paired:
            late = partner(after(b_own, lows[0]), later[:-1], 1)
        if l == 2 and paired:
            b_blocks = [b_own, partner(after(b_own, low), [final])]
            leaving = partner(after(leaving, low))
        if paired:
            before = [own_before, early if l == 1 else late]
        h_new, *parts = section_slice(
            l, n_tp, sec, lows, slots, norm_gain, h_prev, own_rows, before
        )
        hs.append(h_new)
        parts = [parts[0]] + [around(parts[s], -s) for s in range(1, n_tp)]
        if l < final:
            h_prev = onward(after(h_new, *parts[1:]), 0)
        else:
            back = h_new
            for m in later[:-1]:
                back = jnp.where(section == m, hs[m], back)
            back = onward(after(back, *parts[1:]), 0, -1)
        fresh, low = attend_call(
            functools.partial(later_kernel, l, n_tp, n_a, depth),
            [sec, *parts, *shared],
            a_blocks,
            tokens,
            q_width,
            "section_%d" % l,
        )
        news.append(fresh)
    lows = [low] + [around(low, s) for s in range(1, n_tp)]
    fresh = news[0]
    for l in later:
        fresh = jnp.where(section == l, news[l], fresh)
    if paired:
        arrived = insert_new(spots, partner(fresh), leaving)
    else:
        leaving = insert_new(spots, fresh, leaving)[0]
        count = moves.shape[0]
        free_slots = (n_req - 1) * ((count + n_req - 2) // (n_req - 1))
        received, dest_in, spots_in = (
            lax.all_gather(x, "req", axis=0, tiled=True)
            for x in (leaving, moves[:, 0], moves[:, 2])
        )
        target = jnp.where(dest_in == my_req, spots_in, free_slots)
        empty = jnp.zeros((free_slots, *leaving.shape[1:]), jnp.bfloat16)
        arrived = empty.at[target].set(received, mode="drop")[None]
    section_out = section_result(final, n_tp, sec, back, lows, slots, h_new, b_blocks)
    return (section_out, fresh.reshape(1, tokens, 2, HD), arrived)


def solution(mesh):
    in_specs = (
        P("req", "tp"),
        P("pipe", "req", "tp"),
        P("pipe", None),
        P("pipe", None, None, "tp"),
        P("pipe", "req", None, "tp"),
        P("pipe", "req", None, "tp"),
        P("pipe", "req", None, None, "tp"),
        P("req"),
        P(),
        P("req", None),
        P("req"),
        P("req", None),
    )
    out_specs = (
        P("pipe", "req", "tp"),
        P("pipe", "req", None, "tp"),
        P("pipe", "req", None, None, "tp"),
    )
    return jax.shard_map(body, mesh=mesh, in_specs=in_specs, out_specs=out_specs, check_vma=False)
```

```python
import functools
import math

import jax
import jax.numpy as jnp
from jax import lax
from jax.experimental import pallas as pl
from jax.experimental.pallas import tpu as pltpu
from jax.sharding import PartitionSpec as P

HD = 128
R = 64
S = 4
PAGE = 64
MAXP = 4
EPS = 1e-05
BIG = -1e30
VMEM_MIB = 20
SCALE = HD ** (-0.5)
VM = pl.BlockSpec(memory_space=pltpu.VMEM)
SM = pl.BlockSpec(memory_space=pltpu.SMEM)
ANY = pl.BlockSpec(memory_space=pltpu.HBM)
NT = (((1,), (1,)), ((), ()))


def vmem(*large):
    size = sum(x.size * x.dtype.itemsize for x in large)
    return pltpu.CompilerParams(vmem_limit_bytes=(VMEM_MIB << 20) + size)


def kept(shape, dtype):
    return pltpu.VMEM(shape, dtype)


def in_hbm(x):
    return pltpu.with_memory_space_constraint(x, pltpu.HBM)


def cost(micros):
    return pl.CostEstimate(flops=0, bytes_accessed=int(micros * 3_000_000), transcendentals=0)


def sds(shape, dtype):
    return jax.ShapeDtypeStruct(shape, dtype)


def halves_of(rows):
    return rows // 2


def split_kernel(chunks, section_of, sec_ref, *refs):
    raw_refs, (out_ref, buf, wide, sems) = refs[:-4], refs[-4:]
    rows = buf.shape[1] // 2

    @pl.when(section_of(sec_ref[0]))
    def _():
        loads = []
        for index, (source, start, _) in enumerate(chunks):
            first = pl.multiple_of(start(sec_ref) * 2 * rows, 2 * rows)
            loads.append(
                pltpu.make_async_copy(
                    raw_refs[source].at[pl.ds(first, 2 * rows)], buf.at[index], sems.at[index]
                )
            )
            loads[-1].start()
        for index, (_, _, to) in enumerate(chunks):
            loads[index].wait()
            wide[...] = buf[index].astype(jnp.float32)
            out = pl.ds(pl.multiple_of(to(sec_ref) * rows, rows), rows)
            out_ref[out, :HD] = wide[pl.ds(0, rows, stride=2), :].astype(jnp.bfloat16)
            out_ref[out, HD:] = wide[pl.ds(1, rows, stride=2), :].astype(jnp.bfloat16)


def split_parts(sec, raws, chunks, section_of, rows, name):
    return pl.pallas_call(
        functools.partial(split_kernel, chunks, section_of),
        in_specs=[SM] + [ANY] * len(raws),
        out_specs=VM,
        out_shape=kept((rows * len(chunks), 2 * HD), jnp.bfloat16),
        scratch_shapes=[
            pltpu.VMEM((len(chunks), 2 * rows, HD), jnp.bfloat16),
            pltpu.VMEM((2 * rows, HD), jnp.float32),
            pltpu.SemaphoreType.DMA((len(chunks),)),
        ],
        compiler_params=vmem(),
        cost_estimate=cost(0.3),
        name=name,
    )(sec, *[in_hbm(x) for x in raws])


def parcel_kernel(n_tp, sec_ref, h_ref, raw_ref, *refs):
    out_refs, sems = refs[:-1], refs[-1]
    rows = out_refs[0].shape[0]
    width = h_ref.shape[1]

    @pl.when(sec_ref[0] == 0)
    def _():
        for out in out_refs:
            for c in range(width // HD):
                out[c * HD : (c + 1) * HD, :] = h_ref[:, c * HD : (c + 1) * HD]

    @pl.when(sec_ref[0] != 0)
    def _():
        loads = []
        for s in range(1, n_tp):
            place = lax.rem(sec_ref[1] + s, n_tp) * 2 + sec_ref[2]
            first = pl.multiple_of(place * rows, rows)
            loads.append(
                pltpu.make_async_copy(
                    raw_ref.at[pl.ds(first, rows)], out_refs[s - 1], sems.at[s - 1]
                )
            )
            loads[-1].start()
        for load in loads:
            load.wait()


def parcels(sec, hidden, raw, n_tp):
    tokens, width = hidden.shape
    rows = raw.shape[0] // (2 * n_tp)
    assert tokens == HD and rows * HD == tokens * width
    return pl.pallas_call(
        functools.partial(parcel_kernel, n_tp),
        in_specs=[SM, VM, ANY],
        out_specs=(VM,) * (n_tp - 1),
        out_shape=(sds((rows, HD), jnp.bfloat16),) * (n_tp - 1),
        scratch_shapes=[pltpu.SemaphoreType.DMA((n_tp - 1,))],
        compiler_params=vmem(),
        cost_estimate=cost(2),
        name="parcels",
    )(sec, hidden, in_hbm(raw))


def local_kernel(
    paired,
    adapters,
    sec_ref,
    table_ref,
    len_ref,
    ids_ref,
    rows_ref,
    move_ref,
    q_ref,
    pages_ref,
    acc_ref,
    lse_ref,
    slot_ref,
    cos_ref,
    sin_ref,
    leave_ref,
    spot_ref,
    buf,
    place,
    sems,
    leave_sem,
):
    heads, tokens, _ = acc_ref.shape
    reqs = tokens // S
    moves = leave_ref.shape[0]
    per = 16 // S
    ctx = MAXP * PAGE
    pages = per * MAXP

    def start(i, _):
        page = table_ref[i]
        place[page] = i
        pltpu.make_async_copy(pages_ref.at[page], buf.at[i], sems.at[i // pages]).start()
        return 0

    lax.fori_loop(0, reqs * MAXP, start, 0, unroll=8)
    lanes = lax.broadcasted_iota(jnp.int32, (1, tokens), 1)

    def leave(i, _):
        page = move_ref[3 * i + 1]
        to = move_ref[3 * i + 2] if paired else i
        pltpu.make_async_copy(pages_ref.at[page], leave_ref.at[to], leave_sem).start()
        index = place[page]
        req = index // MAXP
        position = len_ref[req] + lanes % S
        hit = (lanes // S == req) & (position // PAGE == index % MAXP)
        spot_ref[pl.ds(to, 1), :] = jnp.where(hit, position % PAGE, -1)
        return 0

    lax.fori_loop(0, moves, leave, 0)

    eight = lax.broadcasted_iota(jnp.int32, (8, HD), 0)
    freq = jnp.exp(
        (-math.log(500000.0) * 2.0 / HD)
        * (lax.broadcasted_iota(jnp.int32, (8, HD), 1) % (HD // 2)).astype(jnp.float32)
    )
    sign = jnp.where(lax.broadcasted_iota(jnp.int32, (8, HD), 1) < HD // 2, -1.0, 1.0)
    for i in range(tokens // 8):
        slot, length = [], []
        for r in (2 * i, 2 * i + 1):
            row = rows_ref[ids_ref[r]]
            if paired:
                away = jnp.where(row // adapters == sec_ref[3], 0, adapters)
                row = row % adapters + away
            slot.append(row)
            length.append(len_ref[r])
        span = slice(8 * i, 8 * i + 8)
        first = eight < S
        slot_ref[span, :] = jnp.where(first, slot[0], slot[1])
        position = jnp.where(first, length[0], length[1]) + eight % S
        angle = position.astype(jnp.float32) * freq
        cos_ref[span, :] = jnp.cos(angle)
        sin_ref[span, :] = jnp.sin(angle) * sign

    lane = lax.broadcasted_iota(jnp.int32, (ctx, HD), 1)
    mine = (lane % 16) // S
    lane16 = lax.broadcasted_iota(jnp.int32, (16, HD), 1)
    key_at = lax.broadcasted_iota(jnp.int32, (ctx, HD), 0)
    row_of = (lax.broadcasted_iota(jnp.int32, (HD, HD), 0) % 16) // S

    def group(g, _):
        first = pl.multiple_of(g * pages, pages)
        block = buf.at[pl.ds(first, pages)]
        pltpu.make_async_copy(block, block, sems.at[g]).wait()
        row = pl.multiple_of(g * 16, 16)
        q = jnp.concatenate(
            [q_ref[pl.ds(row, 16), h * HD : (h + 1) * HD] for h in range(heads)], axis=0
        )
        scores = None
        limit = None
        for r in range(per):
            keys = buf[pl.ds(first + r * MAXP, MAXP), 0].reshape(ctx, HD)
            part = lax.dot_general(keys, q, NT, preferred_element_type=jnp.float32)
            length = len_ref[g * per + r]
            scores = part if r == 0 else jnp.where(mine == r, part, scores)
            limit = length if r == 0 else jnp.where(mine[:1] == r, length, limit)
        scores = jnp.where(key_at < limit, scores * SCALE, BIG)
        top = jnp.max(scores, axis=0, keepdims=True)
        weights = jnp.exp(scores - top)
        total = jnp.sum(weights, axis=0, keepdims=True)
        column = jnp.transpose(jnp.broadcast_to(top + jnp.log(total), (HD, HD)))
        packed = column[:16]
        for h in range(1, heads):
            packed = jnp.where(lane16 == h, column[h * 16 : (h + 1) * 16], packed)
        lse_ref[pl.ds(row, 16), :] = packed
        weights = jnp.transpose(weights * (1.0 / total)).astype(jnp.bfloat16)
        mixed = None
        for r in range(per):
            values = buf[pl.ds(first + r * MAXP, MAXP), 1].reshape(ctx, HD)
            part = jnp.dot(weights, values, preferred_element_type=jnp.float32)
            mixed = part if r == 0 else jnp.where(row_of == r, part, mixed)
        for h in range(heads):
            acc_ref[h, pl.ds(row, 16), :] = mixed[h * 16 : (h + 1) * 16]
        return 0

    lax.fori_loop(0, reqs // per, group, 0, unroll=2)
    pltpu.make_async_copy(leave_ref, leave_ref, leave_sem).wait()


def local_work(paired, adapters, sec, table, lengths, ids, rows, moves, queries, pages):
    tokens, width = queries.shape
    heads = width // HD
    count = moves.shape[0] // 3
    groups = tokens // 16
    square = (tokens, HD)
    return pl.pallas_call(
        functools.partial(local_kernel, paired, adapters),
        in_specs=[SM] * 6 + [VM, ANY],
        out_specs=(VM,) * 7,
        out_shape=(
            kept((heads, tokens, HD), jnp.float32),
            kept(square, jnp.float32),
            kept(square, jnp.int32),
            kept(square, jnp.float32),
            kept(square, jnp.float32),
            sds((count, *pages.shape[1:]), jnp.bfloat16),
            sds((count, tokens), jnp.int32),
        ),
        scratch_shapes=[
            pltpu.VMEM(pages.shape, pages.dtype),
            pltpu.SMEM((pages.shape[0],), jnp.int32),
            pltpu.SemaphoreType.DMA((groups,)),
            pltpu.SemaphoreType.DMA,
        ],
        compiler_params=vmem(),
        cost_estimate=cost(0.3),
        name="local_work",
    )(sec, table, lengths, ids, rows, moves, queries, in_hbm(pages))


def attend_new(proj_k, proj_v, refs, fresh_ref, low_ref, mixed_all, loads):
    q_ref, cos_ref, sin_ref, acc_ref, lse_ref, slot_ref, a_refs = refs
    tokens = proj_k.shape[0]
    heads = q_ref.shape[1] // HD
    keys = (proj_k * cos_ref[...] + pltpu.roll(proj_k, HD // 2, 1) * sin_ref[...]).astype(
        jnp.bfloat16
    )
    values = proj_v.astype(jnp.bfloat16)
    fresh_ref[:, :HD] = keys
    fresh_ref[:, HD:] = values
    rows = lax.broadcasted_iota(jnp.int32, (tokens, tokens), 0)
    cols = lax.broadcasted_iota(jnp.int32, (tokens, tokens), 1)
    allowed = (rows // S == cols // S) & (cols <= rows)
    for h in range(heads):
        span = slice(h * HD, (h + 1) * HD)
        scores = lax.dot_general(q_ref[:, span], keys, NT, preferred_element_type=jnp.float32)
        scores = jnp.where(allowed, scores * SCALE, BIG)
        lse = lse_ref[:, h : h + 1]
        top = jnp.maximum(jnp.max(scores, axis=1, keepdims=True), lse)
        weights = jnp.exp(scores - top)
        old = jnp.exp(lse - top)
        total = jnp.sum(weights, axis=1, keepdims=True) + old
        mixed = jnp.dot(weights.astype(jnp.bfloat16), values, preferred_element_type=jnp.float32)
        mixed_all[:, span] = ((mixed + old * acc_ref[h]) / total).astype(jnp.bfloat16)
    slots = slot_ref[...]
    half = lax.broadcasted_iota(jnp.int32, (tokens, HD), 1) // R
    folded = jnp.zeros((tokens, HD), jnp.float32)
    base = 0
    for a_ref, load in zip(a_refs, loads):
        load.wait()
        low = lax.dot_general(
            mixed_all[...], a_ref[...], NT, preferred_element_type=jnp.float32
        )
        for j in range(a_ref.shape[0] // HD):
            folded = folded + jnp.where(
                slots == base + 2 * j + half, low[:, j * HD : (j + 1) * HD], 0.0
            )
        base += a_ref.shape[0] // R
    folded = folded + pltpu.roll(folded, R, 1)
    low_ref[...] = jnp.where(
        half[: tokens // 2] == 0, folded[: tokens // 2], folded[tokens // 2 :]
    ).astype(jnp.bfloat16)


def start_loads(sources, targets, sems):
    loads = [
        pltpu.make_async_copy(source, target, sems.at[i])
        for i, (source, target) in enumerate(zip(sources, targets))
    ]
    for load in loads:
        load.start()
    return loads


def first_kernel(n_tp, n_a, sec_ref, *refs):
    h_refs, (w_ref, gain_ref) = refs[:n_tp], refs[n_tp : n_tp + 2]
    shared = refs[n_tp + 2 : n_tp + 8]
    a_refs = refs[n_tp + 8 : n_tp + 8 + n_a]
    fresh_ref, low_ref, mixed_all, *a_bufs, sems = refs[n_tp + 8 + n_a :]
    width = h_refs[0].shape[1]

    @pl.when(sec_ref[0] == 0)
    def _():
        loads = start_loads(a_refs, a_bufs, sems)
        tokens = h_refs[0].shape[0]
        proj = jnp.zeros((tokens, 2 * HD), jnp.float32)
        square = jnp.zeros((tokens, 1), jnp.float32)
        for s in range(n_tp):
            place = lax.rem(sec_ref[1] + n_tp - s, n_tp)
            lane = pl.multiple_of(place * width, width)
            row = pl.multiple_of(place * width, width)
            if s == 0:
                h = h_refs[s][...]
            else:
                h = jnp.concatenate(
                    [h_refs[s][c * HD : (c + 1) * HD, :] for c in range(width // HD)], axis=1
                )
            h = h.astype(jnp.float32)
            square = square + jnp.sum(h * h, axis=1, keepdims=True)
            x = (h * gain_ref[:, pl.ds(lane, width)].astype(jnp.float32)).astype(jnp.bfloat16)
            proj = proj + jnp.dot(
                x, w_ref[pl.ds(row, width), :], preferred_element_type=jnp.float32
            )
        proj = proj * lax.rsqrt(square / (n_tp * width) + EPS)
        attend_new(
            proj[:, :HD], proj[:, HD:], (*shared, a_bufs), fresh_ref, low_ref, mixed_all, loads
        )


def later_kernel(section, n_tp, n_a, total_width, sec_ref, held_ref, *refs):
    m_refs = refs[:n_tp]
    shared = refs[n_tp : n_tp + 6]
    a_refs = refs[n_tp + 6 : n_tp + 6 + n_a]
    fresh_ref, low_ref, mixed_all, *a_bufs, sems = refs[n_tp + 6 + n_a :]

    @pl.when(sec_ref[0] != section)
    def _():
        fresh_ref[...] = held_ref[...]

    @pl.when(sec_ref[0] == section)
    def _():
        loads = start_loads(a_refs, a_bufs, sems)
        tokens = fresh_ref.shape[0]
        proj = jnp.zeros((tokens, 2 * HD), jnp.float32)
        square = jnp.zeros((1, HD), jnp.float32)
        for m_ref in m_refs:
            proj = proj + m_ref[:tokens, :].astype(jnp.float32)
            tail = m_ref[tokens : tokens + 16, :HD].astype(jnp.float32)
            square = square + jnp.sum(tail, axis=0, keepdims=True) * 0.125
        inv = lax.rsqrt(square / total_width + EPS)
        inv = jnp.transpose(jnp.broadcast_to(inv, (tokens, HD)))
        attend_new(
            proj[:, :HD] * inv,
            proj[:, HD:] * inv,
            (*shared, a_bufs),
            fresh_ref,
            low_ref,
            mixed_all,
            loads,
        )


def attend_call(kernel, operands, a_blocks, tokens, q_width, name):
    return pl.pallas_call(
        kernel,
        in_specs=[SM] + [VM] * (len(operands) - 1) + [ANY] * len(a_blocks),
        out_specs=(VM, VM),
        out_shape=(
            sds((tokens, 2 * HD), jnp.bfloat16),
            sds((tokens // 2, HD), jnp.bfloat16),
        ),
        scratch_shapes=[
            pltpu.VMEM((tokens, q_width), jnp.bfloat16),
            *[pltpu.VMEM(a.shape, jnp.bfloat16) for a in a_blocks],
            pltpu.SemaphoreType.DMA((len(a_blocks),)),
        ],
        compiler_params=vmem(*a_blocks),
        cost_estimate=cost(5),
        name=name,
    )(*operands, *[in_hbm(a) for a in a_blocks])


def unfold_low(packed, slots, base, rows):
    count = packed.shape[0]
    half = lax.broadcasted_iota(jnp.int32, (count, HD), 1) // R
    turned = pltpu.roll(packed, R, 1)
    low = jnp.concatenate(
        [jnp.where(half == 0, packed, turned), jnp.where(half == 1, packed, turned)], axis=0
    )
    half = lax.broadcasted_iota(jnp.int32, (2 * count, HD), 1) // R
    return jnp.concatenate(
        [
            jnp.where(slots == base + 2 * j + half, low, 0.0).astype(jnp.bfloat16)
            for j in range(rows // HD)
        ],
        axis=1,
    )


def add_delta(low, b_refs, h, span):
    delta = None
    for b_ref, spread in zip(b_refs, low):
        part = jnp.dot(spread, b_ref[:, span], preferred_element_type=jnp.float32)
        delta = part if delta is None else delta + part
    delta = delta.astype(jnp.bfloat16).astype(jnp.float32)
    return (h.astype(jnp.float32) + delta).astype(jnp.bfloat16)


def far_shift(n_tp):
    return n_tp // 2


def spreads(packed, slots, b_refs):
    out = []
    base = 0
    for b_ref in b_refs:
        out.append(unfold_low(packed, slots, base, b_ref.shape[0]))
        base += b_ref.shape[0] // R
    return out


def slice_kernel(section, n_tp, n_b, sec_ref, *refs):
    low_refs = refs[:n_tp]
    slot_ref, gain_ref, near_ref, far_ref, h_ref, held_ref = refs[n_tp : n_tp + 6]
    b_refs = refs[n_tp + 6 : n_tp + 6 + n_b]
    h_out, *m_refs, x_all = refs[n_tp + 6 + n_b :]
    tokens, width = h_ref.shape
    far = far_shift(n_tp)
    part = width // 4

    @pl.when(sec_ref[0] != section)
    def _():
        h_out[...] = held_ref[...]

    @pl.when(sec_ref[0] == section)
    def _():
        packed = low_refs[0][...].astype(jnp.float32)
        for low_ref in low_refs[1:]:
            packed = packed + low_ref[...].astype(jnp.float32)
        rounded = packed.astype(jnp.bfloat16)
        low = spreads(rounded.astype(jnp.float32), slot_ref[...], b_refs)
        square = jnp.zeros((tokens, 1), jnp.float32)
        for c in range(4):
            span = slice(c * part, (c + 1) * part)
            h = add_delta(low, b_refs, h_ref[:, span], span)
            h_out[:, span] = h
            h = h.astype(jnp.float32)
            square = square + jnp.sum(h * h, axis=1, keepdims=True)
            lane = pl.multiple_of(sec_ref[1] * width + c * part, part)
            gain = gain_ref[:, pl.ds(lane, part)].astype(jnp.float32)
            x_all[:, span] = (h * gain).astype(jnp.bfloat16)
        square = jnp.transpose(jnp.broadcast_to(square, (tokens, HD)))[:16]
        high = square.astype(jnp.bfloat16).astype(jnp.float32)
        upper = lax.broadcasted_iota(jnp.int32, (16, HD), 0) < 8
        tail = jnp.where(upper, high, square - high).astype(jnp.bfloat16)
        for s in range(n_tp):
            if s == far:
                rows = far_ref[...]
            else:
                place = s - (s > far)
                rows = near_ref[place * width : (place + 1) * width, :]
            proj = jnp.dot(x_all[...], rows, preferred_element_type=jnp.float32)
            m_refs[s][:tokens, :] = proj.astype(jnp.bfloat16)
            m_refs[s][tokens:, :HD] = tail
            m_refs[s][tokens:, HD:] = jnp.zeros_like(tail)


def section_slice(section, n_tp, sec, lows, slots, gain, near, far, h_prev, held, b_blocks):
    tokens, width = h_prev.shape
    operands = [sec, *lows, slots, gain, near, far, h_prev, held, *b_blocks]
    return pl.pallas_call(
        functools.partial(slice_kernel, section, n_tp, len(b_blocks)),
        in_specs=[SM] + [VM] * (len(operands) - 1),
        out_specs=(VM,) * (1 + n_tp),
        out_shape=(
            sds((tokens, width), jnp.bfloat16),
            *[sds((tokens + 16, 2 * HD), jnp.bfloat16)] * n_tp,
        ),
        scratch_shapes=[pltpu.VMEM((tokens, width), jnp.bfloat16)],
        compiler_params=vmem(*b_blocks),
        cost_estimate=cost(5),
        name="section_slice_%d" % section,
    )(*operands)


def result_kernel(last, n_tp, n_b, sec_ref, back_ref, *refs):
    low_refs = refs[:n_tp]
    slot_ref, h_ref = refs[n_tp : n_tp + 2]
    b_refs = refs[n_tp + 2 : n_tp + 2 + n_b]
    out_ref = refs[n_tp + 2 + n_b]

    @pl.when(sec_ref[0] != last)
    def _():
        out_ref[0] = back_ref[...]

    @pl.when(sec_ref[0] == last)
    def _():
        packed = low_refs[0][...].astype(jnp.float32)
        for low_ref in low_refs[1:]:
            packed = packed + low_ref[...].astype(jnp.float32)
        rounded = packed.astype(jnp.bfloat16).astype(jnp.float32)
        slots = slot_ref[...]
        low = spreads(rounded, slots, b_refs)
        part = h_ref.shape[1] // 4
        for c in range(4):
            span = slice(c * part, (c + 1) * part)
            out_ref[0, :, span] = add_delta(low, b_refs, h_ref[:, span], span)


def section_result(last, n_tp, sec, back, lows, slots, held, b_blocks):
    operands = [sec, back, *lows, slots, held, *b_blocks]
    return pl.pallas_call(
        functools.partial(result_kernel, last, n_tp, len(b_blocks)),
        in_specs=[SM] + [VM] * (len(operands) - 1),
        out_specs=VM,
        out_shape=sds((1, *held.shape), jnp.bfloat16),
        compiler_params=vmem(*b_blocks),
        cost_estimate=cost(3),
        name="section_result",
    )(*operands)


def insert_kernel(spot_ref, new_ref, old_ref, out_ref):
    count = old_ref.shape[0]
    tokens = new_ref.shape[0]
    rows = lax.broadcasted_iota(jnp.int32, (PAGE, tokens), 0)

    def insert(i, _):
        spot = spot_ref[pl.ds(i, 1), :]
        hit = jnp.where(spot == rows, 1.0, 0.0)
        fresh = jnp.sum(hit, axis=1, keepdims=True) > 0.0
        hit = hit.astype(jnp.bfloat16)
        values = jnp.dot(hit, new_ref[...], preferred_element_type=jnp.float32)
        for part in range(2):
            value = values[:, part * HD : (part + 1) * HD]
            old = old_ref[i, part].astype(jnp.float32)
            out_ref[0, i, part] = jnp.where(fresh, value, old).astype(jnp.bfloat16)
        return 0

    lax.fori_loop(0, count, insert, 0, unroll=4)


def insert_new(spots, fresh, old):
    return pl.pallas_call(
        insert_kernel,
        in_specs=[VM] * 3,
        out_specs=VM,
        out_shape=sds((1, *old.shape), jnp.bfloat16),
        compiler_params=vmem(),
        cost_estimate=cost(3),
        name="insert_new",
    )(spots, fresh, old)


def body(
    hidden,
    queries,
    norm_gain,
    kv_weight,
    adapter_in,
    adapter_out,
    kv_pages,
    adapter_ids,
    owner_rows,
    page_table,
    lengths,
    moves,
):
    n_sec, n_req, n_tp = (lax.axis_size(a) for a in ("pipe", "req", "tp"))
    section, my_req, my_tp = (lax.axis_index(a) for a in ("pipe", "req", "tp"))
    tokens, width = hidden.shape
    depth = width * n_tp
    adapters = adapter_in.shape[1]
    q_width = queries.shape[2]

    def around(x, shift):
        return lax.ppermute(x, "tp", [(t, (t + shift) % n_tp) for t in range(n_tp)])

    def onward(x, shift, step=1, sections=range(n_sec)):
        pairs = [
            (l * n_tp + t, (l + step) % n_sec * n_tp + (t + shift) % n_tp)
            for l in sections
            for t in range(n_tp)
        ]
        return lax.ppermute(x, ("pipe", "tp"), pairs)

    def partner(x, sections=range(n_sec), step=0):
        pairs = [
            (l * n_req + i, (l + step) % n_sec * n_req + (i ^ 1))
            for l in sections
            for i in range(n_req)
        ]
        return lax.ppermute(x, ("pipe", "req"), pairs)

    def gather(x):
        return [x, partner(x)] if paired else [lax.all_gather(x, "req", axis=0, tiled=True)]

    def after(x, *others):
        return lax.optimization_barrier((x, *others))[0]

    paired = n_req == 2
    later = list(range(1, n_sec))
    sec = jnp.stack([section, my_tp, my_req % 2, my_req]).astype(jnp.int32)

    a_own = adapter_in[0].reshape(adapters * R, q_width)
    b_own = adapter_out[0].reshape(adapters * R, width)
    raw = kv_weight[0].reshape(2 * depth, HD)
    half = width // 2
    final = n_sec - 1
    sent = parcels(sec, hidden, raw, n_tp)
    mine = [around(sent[s - 1], s) for s in range(1, n_tp)]
    a_blocks = gather(a_own)
    acc, lse, slots, cos, sin, leaving, spots = local_work(
        paired,
        adapters,
        sec,
        page_table.reshape(-1),
        lengths,
        adapter_ids,
        owner_rows,
        moves.reshape(-1),
        queries[0],
        kv_pages[0],
    )
    if paired:
        spots = partner(spots)
        ready = after(b_own, lse)
        own_before = onward(ready, 0)
        early = partner(ready, [0], 1)
    else:
        b_blocks = [lax.all_gather(b_own, "req", axis=0, tiled=True)]
        before = [onward(b_blocks[0], 0)]
    chunks = [(0, lambda sec, i=i: i, lambda sec, i=i: i) for i in range(2 * n_tp)]
    weights = split_parts(
        sec,
        [after(raw, lse, *a_blocks)],
        chunks,
        lambda section: section == 0,
        half,
        "split_first",
    )
    far = far_shift(n_tp)
    turns = [s for s in range(1, n_tp) if s != far]
    other = {s: partner(after(mine[s - 1], lse), later) for s in turns}
    weights = after(weights, *other.values())

    shared = [queries[0], cos, sin, acc, lse, slots]
    n_a = len(a_blocks)
    fresh, low = attend_call(
        functools.partial(first_kernel, n_tp, n_a),
        [sec, hidden, *mine, weights, norm_gain, *shared],
        a_blocks,
        tokens,
        q_width,
        "first_section",
    )
    other[far] = partner(after(mine[far - 1], low), later)
    chunks = [(0, lambda sec, i=i: 2 * sec[1] + i, lambda sec, i=i: i) for i in range(2)]
    raws = [after(raw, low)]
    for place, s in enumerate(turns, 1):
        chunks.append((len(raws), lambda sec: 0, lambda sec, p=place: 2 * p + sec[2]))
        chunks.append((len(raws) + 1, lambda sec: 0, lambda sec, p=place: 2 * p + 1 - sec[2]))
        raws += [mine[s - 1], other[s]]
    inner = lambda section: section > 0
    near_rows = split_parts(sec, raws, chunks, inner, half, "split_near")
    chunks = [(0, lambda sec: 0, lambda sec: sec[2]), (1, lambda sec: 0, lambda sec: 1 - sec[2])]
    far_rows = split_parts(sec, [mine[far - 1], other[far]], chunks, inner, half, "split_far")
    if paired:
        late = partner(after(b_own, near_rows), later[:-1], 1)
    h_prev = h_new = hidden
    for l in later:
        lows = [onward(low, s, 1, [0] if l == 1 else range(n_sec)) for s in range(n_tp)]
        if l == 2 and paired:
            b_blocks = [b_own, partner(after(b_own, low), [final])]
            leaving = partner(after(leaving, low))
        if paired:
            before = [own_before, early if l == 1 else late]
        h_new, *parts = section_slice(
            l, n_tp, sec, lows, slots, norm_gain, near_rows, far_rows, h_prev, h_new, before
        )
        parts = [parts[0]] + [around(parts[s], -s) for s in range(1, n_tp)]
        if l < final:
            h_prev = onward(after(h_new, *parts[1:]), 0)
        else:
            back = onward(after(h_new, *parts[1:]), 0, -1)
        fresh, low = attend_call(
            functools.partial(later_kernel, l, n_tp, n_a, depth),
            [sec, fresh, *parts, *shared],
            a_blocks,
            tokens,
            q_width,
            "section_%d" % l,
        )
    lows = [low] + [around(low, s) for s in range(1, n_tp)]
    if paired:
        arrived = insert_new(spots, partner(fresh), leaving)
    else:
        leaving = insert_new(spots, fresh, leaving)[0]
        count = moves.shape[0]
        free_slots = (n_req - 1) * ((count + n_req - 2) // (n_req - 1))
        received, dest_in, spots_in = (
            lax.all_gather(x, "req", axis=0, tiled=True)
            for x in (leaving, moves[:, 0], moves[:, 2])
        )
        target = jnp.where(dest_in == my_req, spots_in, free_slots)
        empty = jnp.zeros((free_slots, *leaving.shape[1:]), jnp.bfloat16)
        arrived = empty.at[target].set(received, mode="drop")[None]
    section_out = section_result(final, n_tp, sec, back, lows, slots, h_new, b_blocks)
    return (section_out, fresh.reshape(1, tokens, 2, HD), arrived)


def solution(mesh):
    in_specs = (
        P("req", "tp"),
        P("pipe", "req", "tp"),
        P("pipe", None),
        P("pipe", None, None, "tp"),
        P("pipe", "req", None, "tp"),
        P("pipe", "req", None, "tp"),
        P("pipe", "req", None, None, "tp"),
        P("req"),
        P(),
        P("req", None),
        P("req"),
        P("req", None),
    )
    out_specs = (
        P("pipe", "req", "tp"),
        P("pipe", "req", None, "tp"),
        P("pipe", "req", None, None, "tp"),
    )
    return jax.shard_map(body, mesh=mesh, in_specs=in_specs, out_specs=out_specs, check_vma=False)
```

```python
import functools
import math

import jax
import jax.numpy as jnp
from jax import lax
from jax.experimental import pallas as pl
from jax.experimental.pallas import tpu as pltpu
from jax.sharding import PartitionSpec as P

HD = 128
R = 64
S = 4
PAGE = 64
MAXP = 4
EPS = 1e-05
BIG = -1e30
VMEM_MIB = 20
SCALE = HD ** (-0.5)
VM = pl.BlockSpec(memory_space=pltpu.VMEM)
SM = pl.BlockSpec(memory_space=pltpu.SMEM)
ANY = pl.BlockSpec(memory_space=pltpu.HBM)
NT = (((1,), (1,)), ((), ()))


def vmem(*large):
    size = sum(x.size * x.dtype.itemsize for x in large)
    return pltpu.CompilerParams(vmem_limit_bytes=(VMEM_MIB << 20) + size)


def kept(shape, dtype):
    return pltpu.VMEM(shape, dtype)


def in_hbm(x):
    return pltpu.with_memory_space_constraint(x, pltpu.HBM)


def cost(micros):
    return pl.CostEstimate(flops=0, bytes_accessed=int(micros * 3_000_000), transcendentals=0)


def sds(shape, dtype):
    return jax.ShapeDtypeStruct(shape, dtype)


def halves_of(rows):
    return rows // 2


def split_kernel(chunks, section_of, sec_ref, *refs):
    raw_refs, (out_ref, buf, wide, sems) = refs[:-4], refs[-4:]
    rows = buf.shape[1] // 2

    @pl.when(section_of(sec_ref[0]))
    def _():
        loads = []
        for index, (source, start, _) in enumerate(chunks):
            first = pl.multiple_of(start(sec_ref) * 2 * rows, 2 * rows)
            loads.append(
                pltpu.make_async_copy(
                    raw_refs[source].at[pl.ds(first, 2 * rows)], buf.at[index], sems.at[index]
                )
            )
            loads[-1].start()
        for index, (_, _, to) in enumerate(chunks):
            loads[index].wait()
            wide[...] = buf[index].astype(jnp.float32)
            out = pl.ds(pl.multiple_of(to(sec_ref) * rows, rows), rows)
            out_ref[out, :HD] = wide[pl.ds(0, rows, stride=2), :].astype(jnp.bfloat16)
            out_ref[out, HD:] = wide[pl.ds(1, rows, stride=2), :].astype(jnp.bfloat16)


def split_parts(sec, raws, chunks, section_of, rows, name):
    return pl.pallas_call(
        functools.partial(split_kernel, chunks, section_of),
        in_specs=[SM] + [ANY] * len(raws),
        out_specs=VM,
        out_shape=kept((rows * len(chunks), 2 * HD), jnp.bfloat16),
        scratch_shapes=[
            pltpu.VMEM((len(chunks), 2 * rows, HD), jnp.bfloat16),
            pltpu.VMEM((2 * rows, HD), jnp.float32),
            pltpu.SemaphoreType.DMA((len(chunks),)),
        ],
        compiler_params=vmem(),
        cost_estimate=cost(0.3),
        name=name,
    )(sec, *[in_hbm(x) for x in raws])


def parcel_kernel(n_tp, sec_ref, h_ref, raw_ref, *refs):
    out_refs, sems = refs[:-1], refs[-1]
    rows = out_refs[0].shape[0]
    width = h_ref.shape[1]

    @pl.when(sec_ref[0] == 0)
    def _():
        for out in out_refs:
            for c in range(width // HD):
                out[c * HD : (c + 1) * HD, :] = h_ref[:, c * HD : (c + 1) * HD]

    @pl.when(sec_ref[0] != 0)
    def _():
        loads = []
        for s in range(1, n_tp):
            place = lax.rem(sec_ref[1] + s, n_tp) * 2 + sec_ref[2]
            first = pl.multiple_of(place * rows, rows)
            loads.append(
                pltpu.make_async_copy(
                    raw_ref.at[pl.ds(first, rows)], out_refs[s - 1], sems.at[s - 1]
                )
            )
            loads[-1].start()
        for load in loads:
            load.wait()


def parcels(sec, hidden, raw, n_tp):
    tokens, width = hidden.shape
    rows = raw.shape[0] // (2 * n_tp)
    assert tokens == HD and rows * HD == tokens * width
    return pl.pallas_call(
        functools.partial(parcel_kernel, n_tp),
        in_specs=[SM, VM, ANY],
        out_specs=(VM,) * (n_tp - 1),
        out_shape=(sds((rows, HD), jnp.bfloat16),) * (n_tp - 1),
        scratch_shapes=[pltpu.SemaphoreType.DMA((n_tp - 1,))],
        compiler_params=vmem(),
        cost_estimate=cost(2),
        name="parcels",
    )(sec, hidden, in_hbm(raw))


def local_kernel(
    paired,
    adapters,
    sec_ref,
    table_ref,
    len_ref,
    ids_ref,
    rows_ref,
    move_ref,
    q_ref,
    pages_ref,
    acc_out,
    lse_out,
    line_ref,
    slot_ref,
    cos_ref,
    sin_ref,
    leave_ref,
    spot_ref,
    buf,
    place,
    acc_ref,
    lse_ref,
    sems,
    leave_sem,
):
    heads, tokens, _ = acc_ref.shape
    reqs = tokens // S
    moves = leave_ref.shape[0]
    per = 16 // S
    ctx = MAXP * PAGE
    pages = per * MAXP

    def start(i, _):
        page = table_ref[i]
        place[page] = i
        pltpu.make_async_copy(pages_ref.at[page], buf.at[i], sems.at[i // pages]).start()
        return 0

    lax.fori_loop(0, reqs * MAXP, start, 0, unroll=8)
    lanes = lax.broadcasted_iota(jnp.int32, (1, tokens), 1)

    def leave(i, _):
        page = move_ref[3 * i + 1]
        to = move_ref[3 * i + 2] if paired else i
        pltpu.make_async_copy(pages_ref.at[page], leave_ref.at[to], leave_sem).start()
        index = place[page]
        req = index // MAXP
        position = len_ref[req] + lanes % S
        hit = (lanes // S == req) & (position // PAGE == index % MAXP)
        spot_ref[pl.ds(to, 1), :] = jnp.where(hit, position % PAGE, -1)
        return 0

    lax.fori_loop(0, moves, leave, 0)

    eight = lax.broadcasted_iota(jnp.int32, (8, HD), 0)
    freq = jnp.exp(
        (-math.log(500000.0) * 2.0 / HD)
        * (lax.broadcasted_iota(jnp.int32, (8, HD), 1) % (HD // 2)).astype(jnp.float32)
    )
    sign = jnp.where(lax.broadcasted_iota(jnp.int32, (8, HD), 1) < HD // 2, -1.0, 1.0)
    for i in range(tokens // 8):
        slot, length = [], []
        for r in (2 * i, 2 * i + 1):
            row = rows_ref[ids_ref[r]]
            if paired:
                away = jnp.where(row // adapters == sec_ref[3], 0, adapters)
                row = row % adapters + away
            slot.append(row)
            length.append(len_ref[r])
        span = slice(8 * i, 8 * i + 8)
        first = eight < S
        slot_ref[span, :] = jnp.where(first, slot[0], slot[1])
        position = jnp.where(first, length[0], length[1]) + eight % S
        angle = position.astype(jnp.float32) * freq
        cos_ref[span, :] = jnp.cos(angle)
        sin_ref[span, :] = jnp.sin(angle) * sign

    lane = lax.broadcasted_iota(jnp.int32, (ctx, HD), 1)
    mine = (lane % 16) // S
    lane16 = lax.broadcasted_iota(jnp.int32, (16, HD), 1)
    key_at = lax.broadcasted_iota(jnp.int32, (ctx, HD), 0)
    row_of = (lax.broadcasted_iota(jnp.int32, (HD, HD), 0) % 16) // S

    def group(g, _):
        first = pl.multiple_of(g * pages, pages)
        block = buf.at[pl.ds(first, pages)]
        pltpu.make_async_copy(block, block, sems.at[g]).wait()
        row = pl.multiple_of(g * 16, 16)
        q = jnp.concatenate(
            [q_ref[pl.ds(row, 16), h * HD : (h + 1) * HD] for h in range(heads)], axis=0
        )
        scores = None
        limit = None
        for r in range(per):
            keys = buf[pl.ds(first + r * MAXP, MAXP), 0].reshape(ctx, HD)
            part = lax.dot_general(keys, q, NT, preferred_element_type=jnp.float32)
            length = len_ref[g * per + r]
            scores = part if r == 0 else jnp.where(mine == r, part, scores)
            limit = length if r == 0 else jnp.where(mine[:1] == r, length, limit)
        scores = jnp.where(key_at < limit, scores * SCALE, BIG)
        top = jnp.max(scores, axis=0, keepdims=True)
        weights = jnp.exp(scores - top)
        total = jnp.sum(weights, axis=0, keepdims=True)
        column = jnp.transpose(jnp.broadcast_to(top + jnp.log(total), (HD, HD)))
        packed = column[:16]
        for h in range(1, heads):
            packed = jnp.where(lane16 == h, column[h * 16 : (h + 1) * 16], packed)
        lse_ref[pl.ds(row, 16), :] = packed
        weights = jnp.transpose(weights * (1.0 / total)).astype(jnp.bfloat16)
        mixed = None
        for r in range(per):
            values = buf[pl.ds(first + r * MAXP, MAXP), 1].reshape(ctx, HD)
            part = jnp.dot(weights, values, preferred_element_type=jnp.float32)
            mixed = part if r == 0 else jnp.where(row_of == r, part, mixed)
        for h in range(heads):
            acc_ref[h, pl.ds(row, 16), :] = mixed[h * 16 : (h + 1) * 16]
        return 0

    lax.fori_loop(0, reqs // per, group, 0, unroll=2)
    for h in range(heads):
        acc_out[h] = jnp.transpose(acc_ref[h])
    lse_out[...] = jnp.transpose(lse_ref[...])[:heads]
    line_ref[...] = jnp.transpose(slot_ref[...].astype(jnp.float32))[:8]
    pltpu.make_async_copy(leave_ref, leave_ref, leave_sem).wait()


def local_work(paired, adapters, sec, table, lengths, ids, rows, moves, queries, pages):
    tokens, width = queries.shape
    heads = width // HD
    count = moves.shape[0] // 3
    groups = tokens // 16
    square = (tokens, HD)
    return pl.pallas_call(
        functools.partial(local_kernel, paired, adapters),
        in_specs=[SM] * 6 + [VM, ANY],
        out_specs=(VM,) * 8,
        out_shape=(
            kept((heads, HD, tokens), jnp.float32),
            kept((heads, tokens), jnp.float32),
            kept((8, tokens), jnp.float32),
            kept(square, jnp.int32),
            kept(square, jnp.float32),
            kept(square, jnp.float32),
            sds((count, *pages.shape[1:]), jnp.bfloat16),
            sds((count, tokens), jnp.int32),
        ),
        scratch_shapes=[
            pltpu.VMEM(pages.shape, pages.dtype),
            pltpu.SMEM((pages.shape[0],), jnp.int32),
            pltpu.VMEM((heads, tokens, HD), jnp.float32),
            pltpu.VMEM(square, jnp.float32),
            pltpu.SemaphoreType.DMA((groups,)),
            pltpu.SemaphoreType.DMA,
        ],
        compiler_params=vmem(),
        cost_estimate=cost(0.3),
        name="local_work",
    )(sec, table, lengths, ids, rows, moves, queries, in_hbm(pages))


def attend_new(proj_k, proj_v, refs, fresh_ref, low_ref, mixed_all, loads):
    q_ref, cos_ref, sin_ref, acc_ref, lse_ref, slot_ref, spot_ref, a_refs = refs
    tokens = proj_k.shape[0]
    heads = q_ref.shape[1] // HD
    keys = (proj_k * cos_ref[...] + pltpu.roll(proj_k, HD // 2, 1) * sin_ref[...]).astype(
        jnp.bfloat16
    )
    values = proj_v.astype(jnp.bfloat16)
    fresh_ref[:tokens, :HD] = keys
    fresh_ref[:tokens, HD:] = values
    spots = spot_ref[...].astype(jnp.float32).astype(jnp.bfloat16)
    fresh_ref[tokens:, :HD] = spots
    fresh_ref[tokens:, HD:] = jnp.zeros_like(spots)
    values = jnp.transpose(values.astype(jnp.float32)).astype(jnp.bfloat16)
    rows = lax.broadcasted_iota(jnp.int32, (tokens, tokens), 0)
    cols = lax.broadcasted_iota(jnp.int32, (tokens, tokens), 1)
    allowed = (rows // S == cols // S) & (rows <= cols)
    for h in range(heads):
        span = slice(h * HD, (h + 1) * HD)
        scores = lax.dot_general(keys, q_ref[:, span], NT, preferred_element_type=jnp.float32)
        scores = jnp.where(allowed, scores * SCALE, BIG)
        lse = lse_ref[h : h + 1, :]
        top = jnp.maximum(jnp.max(scores, axis=0, keepdims=True), lse)
        weights = jnp.exp(scores - top)
        old = jnp.exp(lse - top)
        share = 1.0 / (jnp.sum(weights, axis=0, keepdims=True) + old)
        weights = (weights * share).astype(jnp.bfloat16)
        mixed = jnp.dot(values, weights, preferred_element_type=jnp.float32)
        mixed_all[span, :] = (mixed + acc_ref[h] * (old * share)).astype(jnp.bfloat16)
    slots = slot_ref[:1, :]
    folded = jnp.zeros((R, tokens), jnp.float32)
    base = 0
    for a_ref, load in zip(a_refs, loads):
        load.wait()
        low = jnp.dot(a_ref[...], mixed_all[...], preferred_element_type=jnp.float32)
        for j in range(a_ref.shape[0] // R):
            folded = folded + jnp.where(slots == float(base + j), low[j * R : (j + 1) * R], 0.0)
        base += a_ref.shape[0] // R
    low_ref[...] = folded.astype(jnp.bfloat16)


def start_loads(sources, targets, sems):
    loads = [
        pltpu.make_async_copy(source, target, sems.at[i])
        for i, (source, target) in enumerate(zip(sources, targets))
    ]
    for load in loads:
        load.start()
    return loads


def first_kernel(n_tp, n_a, sec_ref, *refs):
    h_refs, (w_ref, gain_ref) = refs[:n_tp], refs[n_tp : n_tp + 2]
    shared = refs[n_tp + 2 : n_tp + 9]
    a_refs = refs[n_tp + 9 : n_tp + 9 + n_a]
    fresh_ref, low_ref, mixed_all, *a_bufs, sems = refs[n_tp + 9 + n_a :]
    width = h_refs[0].shape[1]

    @pl.when(sec_ref[0] == 0)
    def _():
        loads = start_loads(a_refs, a_bufs, sems)
        tokens = h_refs[0].shape[0]
        proj = jnp.zeros((tokens, 2 * HD), jnp.float32)
        square = jnp.zeros((tokens, 1), jnp.float32)
        for s in range(n_tp):
            place = lax.rem(sec_ref[1] + n_tp - s, n_tp)
            lane = pl.multiple_of(place * width, width)
            row = pl.multiple_of(place * width, width)
            if h_refs[s].shape[1] == width:
                h = h_refs[s][...]
            else:
                h = jnp.concatenate(
                    [h_refs[s][c * HD : (c + 1) * HD, :] for c in range(width // HD)], axis=1
                )
            h = h.astype(jnp.float32)
            square = square + jnp.sum(h * h, axis=1, keepdims=True)
            x = (h * gain_ref[:, pl.ds(lane, width)].astype(jnp.float32)).astype(jnp.bfloat16)
            proj = proj + jnp.dot(
                x, w_ref[pl.ds(row, width), :], preferred_element_type=jnp.float32
            )
        proj = proj * lax.rsqrt(square / (n_tp * width) + EPS)
        attend_new(
            proj[:, :HD], proj[:, HD:], (*shared, a_bufs), fresh_ref, low_ref, mixed_all, loads
        )


def later_kernel(section, n_tp, n_a, total_width, sec_ref, held_ref, *refs):
    m_refs = refs[:n_tp]
    shared = refs[n_tp : n_tp + 7]
    a_refs = refs[n_tp + 7 : n_tp + 7 + n_a]
    fresh_ref, low_ref, mixed_all, *a_bufs, sems = refs[n_tp + 7 + n_a :]

    @pl.when(sec_ref[0] != section)
    def _():
        fresh_ref[...] = held_ref[...]

    @pl.when(sec_ref[0] == section)
    def _():
        loads = start_loads(a_refs, a_bufs, sems)
        tokens = low_ref.shape[1]
        proj = jnp.zeros((tokens, 2 * HD), jnp.float32)
        square = jnp.zeros((1, HD), jnp.float32)
        for m_ref in m_refs:
            proj = proj + m_ref[:tokens, :].astype(jnp.float32)
            tail = m_ref[tokens : tokens + 16, :HD].astype(jnp.float32)
            square = square + jnp.sum(tail, axis=0, keepdims=True) * 0.125
        inv = lax.rsqrt(square / total_width + EPS)
        inv = jnp.transpose(jnp.broadcast_to(inv, (tokens, HD)))
        attend_new(
            proj[:, :HD] * inv,
            proj[:, HD:] * inv,
            (*shared, a_bufs),
            fresh_ref,
            low_ref,
            mixed_all,
            loads,
        )


def attend_call(kernel, operands, a_blocks, tokens, q_width, name):
    return pl.pallas_call(
        kernel,
        in_specs=[SM] + [VM] * (len(operands) - 1) + [ANY] * len(a_blocks),
        out_specs=(VM, VM),
        out_shape=(
            sds((tokens + 16, 2 * HD), jnp.bfloat16),
            sds((R, tokens), jnp.bfloat16),
        ),
        scratch_shapes=[
            pltpu.VMEM((q_width, tokens), jnp.bfloat16),
            *[pltpu.VMEM(a.shape, jnp.bfloat16) for a in a_blocks],
            pltpu.SemaphoreType.DMA((len(a_blocks),)),
        ],
        compiler_params=vmem(*a_blocks),
        cost_estimate=cost(5),
        name=name,
    )(*operands, *[in_hbm(a) for a in a_blocks])


def unfold_low(packed, slots, base, rows):
    tokens = packed.shape[1]
    low = jnp.transpose(jnp.concatenate([packed, packed], axis=0))
    half = lax.broadcasted_iota(jnp.int32, (tokens, HD), 1) // R
    return jnp.concatenate(
        [
            jnp.where(slots == base + 2 * j + half, low, 0.0).astype(jnp.bfloat16)
            for j in range(rows // HD)
        ],
        axis=1,
    )


def add_delta(low, b_refs, h, span):
    delta = None
    for b_ref, spread in zip(b_refs, low):
        part = jnp.dot(spread, b_ref[:, span], preferred_element_type=jnp.float32)
        delta = part if delta is None else delta + part
    delta = delta.astype(jnp.bfloat16).astype(jnp.float32)
    return (h.astype(jnp.float32) + delta).astype(jnp.bfloat16)


def far_shift(n_tp):
    return n_tp // 2


def spreads(packed, slots, b_refs):
    out = []
    base = 0
    for b_ref in b_refs:
        out.append(unfold_low(packed, slots, base, b_ref.shape[0]))
        base += b_ref.shape[0] // R
    return out


def slice_kernel(section, n_tp, n_b, sec_ref, *refs):
    low_refs = refs[:n_tp]
    slot_ref, gain_ref, near_ref, far_ref, h_ref, held_ref = refs[n_tp : n_tp + 6]
    b_refs = refs[n_tp + 6 : n_tp + 6 + n_b]
    h_out, *m_refs, x_all = refs[n_tp + 6 + n_b :]
    tokens, width = h_ref.shape
    far = far_shift(n_tp)
    part = width // 4

    @pl.when(sec_ref[0] != section)
    def _():
        h_out[...] = held_ref[...]

    @pl.when(sec_ref[0] == section)
    def _():
        packed = low_refs[0][...].astype(jnp.float32)
        for low_ref in low_refs[1:]:
            packed = packed + low_ref[...].astype(jnp.float32)
        rounded = packed.astype(jnp.bfloat16)
        low = spreads(rounded.astype(jnp.float32), slot_ref[...], b_refs)
        square = jnp.zeros((tokens, 1), jnp.float32)
        for c in range(4):
            span = slice(c * part, (c + 1) * part)
            h = add_delta(low, b_refs, h_ref[:, span], span)
            h_out[:, span] = h
            h = h.astype(jnp.float32)
            square = square + jnp.sum(h * h, axis=1, keepdims=True)
            lane = pl.multiple_of(sec_ref[1] * width + c * part, part)
            gain = gain_ref[:, pl.ds(lane, part)].astype(jnp.float32)
            x_all[:, span] = (h * gain).astype(jnp.bfloat16)
        square = jnp.transpose(jnp.broadcast_to(square, (tokens, HD)))[:16]
        high = square.astype(jnp.bfloat16).astype(jnp.float32)
        upper = lax.broadcasted_iota(jnp.int32, (16, HD), 0) < 8
        tail = jnp.where(upper, high, square - high).astype(jnp.bfloat16)
        for s in range(n_tp):
            if s == far:
                rows = far_ref[...]
            else:
                place = s - (s > far)
                rows = near_ref[place * width : (place + 1) * width, :]
            proj = jnp.dot(x_all[...], rows, preferred_element_type=jnp.float32)
            m_refs[s][:tokens, :] = proj.astype(jnp.bfloat16)
            m_refs[s][tokens:, :HD] = tail
            m_refs[s][tokens:, HD:] = jnp.zeros_like(tail)


def section_slice(section, n_tp, sec, lows, slots, gain, near, far, h_prev, held, b_blocks):
    tokens, width = h_prev.shape
    operands = [sec, *lows, slots, gain, near, far, h_prev, held, *b_blocks]
    return pl.pallas_call(
        functools.partial(slice_kernel, section, n_tp, len(b_blocks)),
        in_specs=[SM] + [VM] * (len(operands) - 1),
        out_specs=(VM,) * (1 + n_tp),
        out_shape=(
            sds((tokens, width), jnp.bfloat16),
            *[sds((tokens + 16, 2 * HD), jnp.bfloat16)] * n_tp,
        ),
        scratch_shapes=[pltpu.VMEM((tokens, width), jnp.bfloat16)],
        compiler_params=vmem(*b_blocks),
        cost_estimate=cost(5),
        name="section_slice_%d" % section,
    )(*operands)


def result_kernel(last, n_tp, n_b, sec_ref, back_ref, *refs):
    low_refs = refs[:n_tp]
    slot_ref, h_ref = refs[n_tp : n_tp + 2]
    b_refs = refs[n_tp + 2 : n_tp + 2 + n_b]
    out_ref = refs[n_tp + 2 + n_b]

    @pl.when(sec_ref[0] != last)
    def _():
        out_ref[0] = back_ref[...]

    @pl.when(sec_ref[0] == last)
    def _():
        packed = low_refs[0][...].astype(jnp.float32)
        for low_ref in low_refs[1:]:
            packed = packed + low_ref[...].astype(jnp.float32)
        rounded = packed.astype(jnp.bfloat16).astype(jnp.float32)
        slots = slot_ref[...]
        low = spreads(rounded, slots, b_refs)
        part = h_ref.shape[1] // 4
        for c in range(4):
            span = slice(c * part, (c + 1) * part)
            out_ref[0, :, span] = add_delta(low, b_refs, h_ref[:, span], span)


def section_result(last, n_tp, sec, back, lows, slots, held, b_blocks):
    operands = [sec, back, *lows, slots, held, *b_blocks]
    return pl.pallas_call(
        functools.partial(result_kernel, last, n_tp, len(b_blocks)),
        in_specs=[SM] + [VM] * (len(operands) - 1),
        out_specs=VM,
        out_shape=sds((1, *held.shape), jnp.bfloat16),
        compiler_params=vmem(*b_blocks),
        cost_estimate=cost(3),
        name="section_result",
    )(*operands)


def insert_kernel(new_ref, old_ref, out_ref, spot_ref):
    count = old_ref.shape[0]
    tokens = new_ref.shape[0] - count
    rows = lax.broadcasted_iota(jnp.int32, (PAGE, tokens), 0).astype(jnp.float32)
    spot_ref[...] = new_ref[tokens:, :HD].astype(jnp.float32)

    def insert(i, _):
        hit = jnp.where(spot_ref[pl.ds(i, 1), :] == rows, 1.0, 0.0)
        fresh = jnp.sum(hit, axis=1, keepdims=True) > 0.0
        hit = hit.astype(jnp.bfloat16)
        values = jnp.dot(hit, new_ref[:tokens, :], preferred_element_type=jnp.float32)
        for part in range(2):
            value = values[:, part * HD : (part + 1) * HD]
            old = old_ref[i, part].astype(jnp.float32)
            out_ref[0, i, part] = jnp.where(fresh, value, old).astype(jnp.bfloat16)
        return 0

    lax.fori_loop(0, count, insert, 0, unroll=4)


def insert_new(fresh, old):
    return pl.pallas_call(
        insert_kernel,
        in_specs=[VM] * 2,
        out_specs=VM,
        out_shape=sds((1, *old.shape), jnp.bfloat16),
        scratch_shapes=[pltpu.VMEM((old.shape[0], HD), jnp.float32)],
        compiler_params=vmem(),
        cost_estimate=cost(3),
        name="insert_new",
    )(fresh, old)


def body(
    hidden,
    queries,
    norm_gain,
    kv_weight,
    adapter_in,
    adapter_out,
    kv_pages,
    adapter_ids,
    owner_rows,
    page_table,
    lengths,
    moves,
):
    n_sec, n_req, n_tp = (lax.axis_size(a) for a in ("pipe", "req", "tp"))
    section, my_req, my_tp = (lax.axis_index(a) for a in ("pipe", "req", "tp"))
    tokens, width = hidden.shape
    depth = width * n_tp
    adapters = adapter_in.shape[1]
    q_width = queries.shape[2]

    def around(x, shift, sections=range(n_sec)):
        pairs = [
            (l * n_tp + t, l * n_tp + (t + shift) % n_tp) for l in sections for t in range(n_tp)
        ]
        return lax.ppermute(x, ("pipe", "tp"), pairs)

    def onward(x, shift, step=1, sections=range(n_sec)):
        pairs = [
            (l * n_tp + t, (l + step) % n_sec * n_tp + (t + shift) % n_tp)
            for l in sections
            for t in range(n_tp)
        ]
        return lax.ppermute(x, ("pipe", "tp"), pairs)

    def partner(x, sections=range(n_sec), step=0):
        pairs = [
            (l * n_req + i, (l + step) % n_sec * n_req + (i ^ 1))
            for l in sections
            for i in range(n_req)
        ]
        return lax.ppermute(x, ("pipe", "req"), pairs)

    def gather(x):
        return [x, partner(x)] if paired else [lax.all_gather(x, "req", axis=0, tiled=True)]

    def after(x, *others):
        return lax.optimization_barrier((x, *others))[0]

    paired = n_req == 2
    assert tokens == HD and moves.shape[0] == 16
    later = list(range(1, n_sec))
    sec = jnp.stack([section, my_tp, my_req % 2, my_req]).astype(jnp.int32)

    a_own = adapter_in[0].reshape(adapters * R, q_width)
    b_own = adapter_out[0].reshape(adapters * R, width)
    raw = kv_weight[0].reshape(2 * depth, HD)
    half = width // 2
    final = n_sec - 1
    sent = parcels(sec, hidden, raw, n_tp)
    far = far_shift(n_tp)
    turns = [s for s in range(1, n_tp) if s != far]
    detour = n_sec // 2
    passing = around(hidden, far, [detour])
    mine = {s: around(sent[s - 1], s) for s in turns}
    mine[far] = around(sent[far - 1], far, [1])
    rows_in = [hidden] + [mine[s] for s in range(1, n_tp)]
    rows_in[far] = onward(passing, 0, n_sec - detour, [detour])
    mine_late = around(after(sent[far - 1], *[mine[s] for s in turns]), far, later[1:])
    a_blocks = gather(a_own)
    b_blocks = gather(b_own)
    acc, lse, line, slots, cos, sin, leaving, spots = local_work(
        paired,
        adapters,
        sec,
        page_table.reshape(-1),
        lengths,
        adapter_ids,
        owner_rows,
        moves.reshape(-1),
        queries[0],
        kv_pages[0],
    )
    if paired:
        ready = after(b_own, lse)
        before = [onward(x, 0, 1, range(final)) for x in (ready, b_blocks[1])]
    else:
        before = [onward(b_blocks[0], 0)]
    chunks = [(0, lambda sec, i=i: i, lambda sec, i=i: i) for i in range(2 * n_tp)]
    weights = split_parts(
        sec,
        [after(raw, lse, *a_blocks, *b_blocks)],
        chunks,
        lambda section: section == 0,
        half,
        "split_first",
    )
    other = {s: partner(after(mine[s], lse), later) for s in turns}
    weights = after(weights, *other.values())

    shared = [queries[0], cos, sin, acc, lse, line, spots]
    n_a = len(a_blocks)
    fresh, low = attend_call(
        functools.partial(first_kernel, n_tp, n_a),
        [sec, *rows_in, weights, norm_gain, *shared],
        a_blocks,
        tokens,
        q_width,
        "first_section",
    )
    other[far] = partner(mine[far], [1])
    other_late = partner(mine_late, later[1:])
    chunks = [(0, lambda sec, i=i: 2 * sec[1] + i, lambda sec, i=i: i) for i in range(2)]
    raws = [after(raw, low)]
    for place, s in enumerate(turns, 1):
        chunks.append((len(raws), lambda sec: 0, lambda sec, p=place: 2 * p + sec[2]))
        chunks.append((len(raws) + 1, lambda sec: 0, lambda sec, p=place: 2 * p + 1 - sec[2]))
        raws += [mine[s], other[s]]
    inner = lambda section: section > 0
    near_rows = split_parts(sec, raws, chunks, inner, half, "split_near")
    chunks = [(0, lambda sec: 0, lambda sec: sec[2]), (1, lambda sec: 0, lambda sec: 1 - sec[2])]
    far_rows = split_parts(
        sec, [mine[far], other[far]], chunks, lambda section: section == 1, half, "split_far"
    )
    far_late = split_parts(
        sec, [mine_late, other_late], chunks, lambda section: section > 1, half, "split_far_late"
    )
    h_prev = h_new = hidden
    for l in later:
        lows = [onward(low, s, 1, [0] if l == 1 else range(n_sec)) for s in range(n_tp)]
        if l == 2 and paired:
            leaving = partner(after(leaving, low))
        h_new, *parts = section_slice(
            l,
            n_tp,
            sec,
            lows,
            slots,
            norm_gain,
            near_rows,
            far_rows if l == 1 else far_late,
            h_prev,
            h_new,
            before,
        )
        parts = [parts[0]] + [around(parts[s], -s) for s in range(1, n_tp)]
        if l < final:
            h_prev = onward(after(h_new, *parts[1:]), 0)
        else:
            back = onward(after(h_new, *parts[1:]), 0, -1)
        fresh, low = attend_call(
            functools.partial(later_kernel, l, n_tp, n_a, depth),
            [sec, fresh, *parts, *shared],
            a_blocks,
            tokens,
            q_width,
            "section_%d" % l,
        )
    lows = [low] + [around(low, s) for s in range(1, n_tp)]
    if paired:
        arrived = insert_new(partner(fresh), leaving)
    else:
        leaving = insert_new(fresh, leaving)[0]
        count = moves.shape[0]
        free_slots = (n_req - 1) * ((count + n_req - 2) // (n_req - 1))
        received, dest_in, spots_in = (
            lax.all_gather(x, "req", axis=0, tiled=True)
            for x in (leaving, moves[:, 0], moves[:, 2])
        )
        target = jnp.where(dest_in == my_req, spots_in, free_slots)
        empty = jnp.zeros((free_slots, *leaving.shape[1:]), jnp.bfloat16)
        arrived = empty.at[target].set(received, mode="drop")[None]
    section_out = section_result(final, n_tp, sec, back, lows, slots, h_new, b_blocks)
    return (section_out, fresh[:tokens].reshape(1, tokens, 2, HD), arrived)


def solution(mesh):
    in_specs = (
        P("req", "tp"),
        P("pipe", "req", "tp"),
        P("pipe", None),
        P("pipe", None, None, "tp"),
        P("pipe", "req", None, "tp"),
        P("pipe", "req", None, "tp"),
        P("pipe", "req", None, None, "tp"),
        P("req"),
        P(),
        P("req", None),
        P("req"),
        P("req", None),
    )
    out_specs = (
        P("pipe", "req", "tp"),
        P("pipe", "req", None, "tp"),
        P("pipe", "req", None, None, "tp"),
    )
    return jax.shard_map(body, mesh=mesh, in_specs=in_specs, out_specs=out_specs, check_vma=False)
```

```python
import functools
import math

import jax
import jax.numpy as jnp
from jax import lax
from jax.experimental import pallas as pl
from jax.experimental.pallas import tpu as pltpu
from jax.sharding import PartitionSpec as P

HD = 128
R = 64
S = 4
PAGE = 64
MAXP = 4
EPS = 1e-05
BIG = -1e30
VMEM_MIB = 20
SCALE = HD ** (-0.5)
VM = pl.BlockSpec(memory_space=pltpu.VMEM)
SM = pl.BlockSpec(memory_space=pltpu.SMEM)
ANY = pl.BlockSpec(memory_space=pltpu.HBM)
NT = (((1,), (1,)), ((), ()))


def vmem(*large):
    size = sum(x.size * x.dtype.itemsize for x in large)
    return pltpu.CompilerParams(vmem_limit_bytes=(VMEM_MIB << 20) + size)


def kept(shape, dtype):
    return pltpu.VMEM(shape, dtype)


def in_hbm(x):
    return pltpu.with_memory_space_constraint(x, pltpu.HBM)


def cost(micros):
    return pl.CostEstimate(flops=0, bytes_accessed=int(micros * 3_000_000), transcendentals=0)


def sds(shape, dtype):
    return jax.ShapeDtypeStruct(shape, dtype)


def halves_of(rows):
    return rows // 2


def split_kernel(chunks, section_of, sec_ref, *refs):
    raw_refs, (out_ref, buf, wide, sems) = refs[:-4], refs[-4:]
    rows = buf.shape[1] // 2

    @pl.when(section_of(sec_ref[0]))
    def _():
        loads = []
        for index, (source, start, _) in enumerate(chunks):
            first = pl.multiple_of(start(sec_ref) * 2 * rows, 2 * rows)
            loads.append(
                pltpu.make_async_copy(
                    raw_refs[source].at[pl.ds(first, 2 * rows)], buf.at[index], sems.at[index]
                )
            )
            loads[-1].start()
        for index, (_, _, to) in enumerate(chunks):
            loads[index].wait()
            wide[...] = buf[index].astype(jnp.float32)
            out = pl.ds(pl.multiple_of(to(sec_ref) * rows, rows), rows)
            out_ref[out, :HD] = wide[pl.ds(0, rows, stride=2), :].astype(jnp.bfloat16)
            out_ref[out, HD:] = wide[pl.ds(1, rows, stride=2), :].astype(jnp.bfloat16)


def split_parts(sec, raws, chunks, section_of, rows, name):
    return pl.pallas_call(
        functools.partial(split_kernel, chunks, section_of),
        in_specs=[SM] + [ANY] * len(raws),
        out_specs=VM,
        out_shape=kept((rows * len(chunks), 2 * HD), jnp.bfloat16),
        scratch_shapes=[
            pltpu.VMEM((len(chunks), 2 * rows, HD), jnp.bfloat16),
            pltpu.VMEM((2 * rows, HD), jnp.float32),
            pltpu.SemaphoreType.DMA((len(chunks),)),
        ],
        compiler_params=vmem(),
        cost_estimate=cost(0.3),
        name=name,
    )(sec, *[in_hbm(x) for x in raws])


def parcel_kernel(n_tp, sec_ref, h_ref, raw_ref, *refs):
    out_refs, sems = refs[:-1], refs[-1]
    rows = out_refs[0].shape[0]
    width = h_ref.shape[1]

    @pl.when(sec_ref[0] == 0)
    def _():
        for out in out_refs:
            for c in range(width // HD):
                out[c * HD : (c + 1) * HD, :] = h_ref[:, c * HD : (c + 1) * HD]

    @pl.when(sec_ref[0] != 0)
    def _():
        loads = []
        for s in range(1, n_tp):
            place = lax.rem(sec_ref[1] + s, n_tp) * 2 + sec_ref[2]
            first = pl.multiple_of(place * rows, rows)
            loads.append(
                pltpu.make_async_copy(
                    raw_ref.at[pl.ds(first, rows)], out_refs[s - 1], sems.at[s - 1]
                )
            )
            loads[-1].start()
        for load in loads:
            load.wait()


def parcels(sec, hidden, raw, n_tp):
    tokens, width = hidden.shape
    rows = raw.shape[0] // (2 * n_tp)
    assert tokens == HD and rows * HD == tokens * width
    return pl.pallas_call(
        functools.partial(parcel_kernel, n_tp),
        in_specs=[SM, VM, ANY],
        out_specs=(VM,) * (n_tp - 1),
        out_shape=(sds((rows, HD), jnp.bfloat16),) * (n_tp - 1),
        scratch_shapes=[pltpu.SemaphoreType.DMA((n_tp - 1,))],
        compiler_params=vmem(),
        cost_estimate=cost(2),
        name="parcels",
    )(sec, hidden, in_hbm(raw))


def local_kernel(
    paired,
    adapters,
    sec_ref,
    table_ref,
    len_ref,
    ids_ref,
    rows_ref,
    move_ref,
    q_ref,
    pages_ref,
    acc_out,
    lse_out,
    line_ref,
    slot_ref,
    cos_ref,
    sin_ref,
    leave_ref,
    spot_ref,
    buf,
    place,
    acc_ref,
    lse_ref,
    sems,
    leave_sem,
):
    heads, tokens, _ = acc_ref.shape
    reqs = tokens // S
    moves = leave_ref.shape[0]
    per = 16 // S
    ctx = MAXP * PAGE
    pages = per * MAXP

    def start(i, _):
        page = table_ref[i]
        place[page] = i
        pltpu.make_async_copy(pages_ref.at[page], buf.at[i], sems.at[i // pages]).start()
        return 0

    lax.fori_loop(0, reqs * MAXP, start, 0, unroll=8)
    lanes = lax.broadcasted_iota(jnp.int32, (1, tokens), 1)

    def leave(i, _):
        page = move_ref[3 * i + 1]
        to = move_ref[3 * i + 2] if paired else i
        pltpu.make_async_copy(pages_ref.at[page], leave_ref.at[to], leave_sem).start()
        index = place[page]
        req = index // MAXP
        position = len_ref[req] + lanes % S
        hit = (lanes // S == req) & (position // PAGE == index % MAXP)
        spot_ref[pl.ds(to, 1), :] = jnp.where(hit, position % PAGE, -1)
        return 0

    lax.fori_loop(0, moves, leave, 0)

    eight = lax.broadcasted_iota(jnp.int32, (8, HD), 0)
    freq = jnp.exp(
        (-math.log(500000.0) * 2.0 / HD)
        * (lax.broadcasted_iota(jnp.int32, (8, HD), 1) % (HD // 2)).astype(jnp.float32)
    )
    sign = jnp.where(lax.broadcasted_iota(jnp.int32, (8, HD), 1) < HD // 2, -1.0, 1.0)
    for i in range(tokens // 8):
        slot, length = [], []
        for r in (2 * i, 2 * i + 1):
            row = rows_ref[ids_ref[r]]
            if paired:
                away = jnp.where(row // adapters == sec_ref[3], 0, adapters)
                row = row % adapters + away
            slot.append(row)
            length.append(len_ref[r])
        span = slice(8 * i, 8 * i + 8)
        first = eight < S
        slot_ref[span, :] = jnp.where(first, slot[0], slot[1])
        position = jnp.where(first, length[0], length[1]) + eight % S
        angle = position.astype(jnp.float32) * freq
        cos_ref[span, :] = jnp.cos(angle)
        sin_ref[span, :] = jnp.sin(angle) * sign

    lane = lax.broadcasted_iota(jnp.int32, (ctx, HD), 1)
    mine = (lane % 16) // S
    lane16 = lax.broadcasted_iota(jnp.int32, (16, HD), 1)
    key_at = lax.broadcasted_iota(jnp.int32, (ctx, HD), 0)
    row_of = (lax.broadcasted_iota(jnp.int32, (HD, HD), 0) % 16) // S

    def group(g, _):
        first = pl.multiple_of(g * pages, pages)
        block = buf.at[pl.ds(first, pages)]
        pltpu.make_async_copy(block, block, sems.at[g]).wait()
        row = pl.multiple_of(g * 16, 16)
        q = jnp.concatenate(
            [q_ref[pl.ds(row, 16), h * HD : (h + 1) * HD] for h in range(heads)], axis=0
        )
        scores = None
        limit = None
        for r in range(per):
            keys = buf[pl.ds(first + r * MAXP, MAXP), 0].reshape(ctx, HD)
            part = lax.dot_general(keys, q, NT, preferred_element_type=jnp.float32)
            length = len_ref[g * per + r]
            scores = part if r == 0 else jnp.where(mine == r, part, scores)
            limit = length if r == 0 else jnp.where(mine[:1] == r, length, limit)
        scores = jnp.where(key_at < limit, scores * SCALE, BIG)
        top = jnp.max(scores, axis=0, keepdims=True)
        weights = jnp.exp(scores - top)
        total = jnp.sum(weights, axis=0, keepdims=True)
        column = jnp.transpose(jnp.broadcast_to(top + jnp.log(total), (HD, HD)))
        packed = column[:16]
        for h in range(1, heads):
            packed = jnp.where(lane16 == h, column[h * 16 : (h + 1) * 16], packed)
        lse_ref[pl.ds(row, 16), :] = packed
        weights = jnp.transpose(weights * (1.0 / total)).astype(jnp.bfloat16)
        mixed = None
        for r in range(per):
            values = buf[pl.ds(first + r * MAXP, MAXP), 1].reshape(ctx, HD)
            part = jnp.dot(weights, values, preferred_element_type=jnp.float32)
            mixed = part if r == 0 else jnp.where(row_of == r, part, mixed)
        for h in range(heads):
            acc_ref[h, pl.ds(row, 16), :] = mixed[h * 16 : (h + 1) * 16]
        return 0

    lax.fori_loop(0, reqs // per, group, 0, unroll=2)
    for h in range(heads):
        acc_out[h] = jnp.transpose(acc_ref[h])
    lse_out[...] = jnp.transpose(lse_ref[...])[:heads]
    line_ref[...] = jnp.transpose(slot_ref[...].astype(jnp.float32))[:8]
    pltpu.make_async_copy(leave_ref, leave_ref, leave_sem).wait()


def local_work(paired, adapters, sec, table, lengths, ids, rows, moves, queries, pages):
    tokens, width = queries.shape
    heads = width // HD
    count = moves.shape[0] // 3
    groups = tokens // 16
    square = (tokens, HD)
    return pl.pallas_call(
        functools.partial(local_kernel, paired, adapters),
        in_specs=[SM] * 6 + [VM, ANY],
        out_specs=(VM,) * 8,
        out_shape=(
            kept((heads, HD, tokens), jnp.float32),
            kept((heads, tokens), jnp.float32),
            kept((8, tokens), jnp.float32),
            kept(square, jnp.int32),
            kept(square, jnp.float32),
            kept(square, jnp.float32),
            sds((count, *pages.shape[1:]), jnp.bfloat16),
            sds((count, tokens), jnp.int32),
        ),
        scratch_shapes=[
            pltpu.VMEM(pages.shape, pages.dtype),
            pltpu.SMEM((pages.shape[0],), jnp.int32),
            pltpu.VMEM((heads, tokens, HD), jnp.float32),
            pltpu.VMEM(square, jnp.float32),
            pltpu.SemaphoreType.DMA((groups,)),
            pltpu.SemaphoreType.DMA,
        ],
        compiler_params=vmem(),
        cost_estimate=cost(0.3),
        name="local_work",
    )(sec, table, lengths, ids, rows, moves, queries, in_hbm(pages))


def attend_new(proj_k, proj_v, refs, fresh_ref, low_ref, mixed_all, loads):
    q_ref, cos_ref, sin_ref, acc_ref, lse_ref, slot_ref, spot_ref, a_refs = refs
    tokens = proj_k.shape[0]
    heads = q_ref.shape[1] // HD
    keys = (proj_k * cos_ref[...] + pltpu.roll(proj_k, HD // 2, 1) * sin_ref[...]).astype(
        jnp.bfloat16
    )
    values = proj_v.astype(jnp.bfloat16)
    fresh_ref[:tokens, :HD] = keys
    fresh_ref[:tokens, HD:] = values
    spots = spot_ref[...].astype(jnp.float32).astype(jnp.bfloat16)
    fresh_ref[tokens:, :HD] = spots
    fresh_ref[tokens:, HD:] = jnp.zeros_like(spots)
    values = jnp.transpose(values.astype(jnp.float32)).astype(jnp.bfloat16)
    rows = lax.broadcasted_iota(jnp.int32, (tokens, tokens), 0)
    cols = lax.broadcasted_iota(jnp.int32, (tokens, tokens), 1)
    allowed = (rows // S == cols // S) & (rows <= cols)
    for h in range(heads):
        span = slice(h * HD, (h + 1) * HD)
        scores = lax.dot_general(keys, q_ref[:, span], NT, preferred_element_type=jnp.float32)
        scores = jnp.where(allowed, scores * SCALE, BIG)
        lse = lse_ref[h : h + 1, :]
        top = jnp.maximum(jnp.max(scores, axis=0, keepdims=True), lse)
        weights = jnp.exp(scores - top)
        old = jnp.exp(lse - top)
        share = 1.0 / (jnp.sum(weights, axis=0, keepdims=True) + old)
        weights = (weights * share).astype(jnp.bfloat16)
        mixed = jnp.dot(values, weights, preferred_element_type=jnp.float32)
        mixed_all[span, :] = (mixed + acc_ref[h] * (old * share)).astype(jnp.bfloat16)
    slots = slot_ref[:1, :]
    folded = jnp.zeros((R, tokens), jnp.float32)
    base = 0
    for a_ref, load in zip(a_refs, loads):
        load.wait()
        low = jnp.dot(a_ref[...], mixed_all[...], preferred_element_type=jnp.float32)
        for j in range(a_ref.shape[0] // R):
            folded = folded + jnp.where(slots == float(base + j), low[j * R : (j + 1) * R], 0.0)
        base += a_ref.shape[0] // R
    low_ref[...] = folded.astype(jnp.bfloat16)


def start_loads(sources, targets, sems):
    loads = [
        pltpu.make_async_copy(source, target, sems.at[i])
        for i, (source, target) in enumerate(zip(sources, targets))
    ]
    for load in loads:
        load.start()
    return loads


def first_kernel(n_tp, n_a, sec_ref, *refs):
    h_refs, (w_ref, gain_ref) = refs[:n_tp], refs[n_tp : n_tp + 2]
    shared = refs[n_tp + 2 : n_tp + 9]
    a_refs = refs[n_tp + 9 : n_tp + 9 + n_a]
    fresh_ref, low_ref, mixed_all, *a_bufs, sems = refs[n_tp + 9 + n_a :]
    width = h_refs[0].shape[1]

    @pl.when(sec_ref[0] == 0)
    def _():
        loads = start_loads(a_refs, a_bufs, sems)
        tokens = h_refs[0].shape[0]
        proj = jnp.zeros((tokens, 2 * HD), jnp.float32)
        square = jnp.zeros((tokens, 1), jnp.float32)
        for s in range(n_tp):
            place = lax.rem(sec_ref[1] + n_tp - s, n_tp)
            lane = pl.multiple_of(place * width, width)
            row = pl.multiple_of(place * width, width)
            if h_refs[s].shape[1] == width:
                h = h_refs[s][...]
            else:
                h = jnp.concatenate(
                    [h_refs[s][c * HD : (c + 1) * HD, :] for c in range(width // HD)], axis=1
                )
            h = h.astype(jnp.float32)
            square = square + jnp.sum(h * h, axis=1, keepdims=True)
            x = (h * gain_ref[:, pl.ds(lane, width)].astype(jnp.float32)).astype(jnp.bfloat16)
            proj = proj + jnp.dot(
                x, w_ref[pl.ds(row, width), :], preferred_element_type=jnp.float32
            )
        proj = proj * lax.rsqrt(square / (n_tp * width) + EPS)
        attend_new(
            proj[:, :HD], proj[:, HD:], (*shared, a_bufs), fresh_ref, low_ref, mixed_all, loads
        )


def later_kernel(section, n_tp, n_a, total_width, sec_ref, held_ref, *refs):
    m_refs = refs[:n_tp]
    shared = refs[n_tp : n_tp + 7]
    a_refs = refs[n_tp + 7 : n_tp + 7 + n_a]
    fresh_ref, low_ref, mixed_all, *a_bufs, sems = refs[n_tp + 7 + n_a :]

    @pl.when(sec_ref[0] != section)
    def _():
        fresh_ref[...] = held_ref[...]

    @pl.when(sec_ref[0] == section)
    def _():
        loads = start_loads(a_refs, a_bufs, sems)
        tokens = low_ref.shape[1]
        proj = jnp.zeros((tokens, 2 * HD), jnp.float32)
        square = jnp.zeros((1, HD), jnp.float32)
        for m_ref in m_refs:
            proj = proj + m_ref[:tokens, :].astype(jnp.float32)
            tail = m_ref[tokens : tokens + 16, :HD].astype(jnp.float32)
            square = square + jnp.sum(tail, axis=0, keepdims=True) * 0.125
        inv = lax.rsqrt(square / total_width + EPS)
        inv = jnp.transpose(jnp.broadcast_to(inv, (tokens, HD)))
        attend_new(
            proj[:, :HD] * inv,
            proj[:, HD:] * inv,
            (*shared, a_bufs),
            fresh_ref,
            low_ref,
            mixed_all,
            loads,
        )


def attend_call(kernel, operands, a_blocks, tokens, q_width, name):
    return pl.pallas_call(
        kernel,
        in_specs=[SM] + [VM] * (len(operands) - 1) + [ANY] * len(a_blocks),
        out_specs=(VM, VM),
        out_shape=(
            sds((tokens + 16, 2 * HD), jnp.bfloat16),
            sds((R, tokens), jnp.bfloat16),
        ),
        scratch_shapes=[
            pltpu.VMEM((q_width, tokens), jnp.bfloat16),
            *[pltpu.VMEM(a.shape, jnp.bfloat16) for a in a_blocks],
            pltpu.SemaphoreType.DMA((len(a_blocks),)),
        ],
        compiler_params=vmem(*a_blocks),
        cost_estimate=cost(5),
        name=name,
    )(*operands, *[in_hbm(a) for a in a_blocks])


def unfold_low(packed, slots, base, rows):
    tokens = packed.shape[1]
    low = jnp.transpose(jnp.concatenate([packed, packed], axis=0))
    half = lax.broadcasted_iota(jnp.int32, (tokens, HD), 1) // R
    return jnp.concatenate(
        [
            jnp.where(slots == base + 2 * j + half, low, 0.0).astype(jnp.bfloat16)
            for j in range(rows // HD)
        ],
        axis=1,
    )


def add_delta(low, b_refs, h, span):
    delta = None
    for b_ref, spread in zip(b_refs, low):
        part = jnp.dot(spread, b_ref[:, span], preferred_element_type=jnp.float32)
        delta = part if delta is None else delta + part
    delta = delta.astype(jnp.bfloat16).astype(jnp.float32)
    return (h.astype(jnp.float32) + delta).astype(jnp.bfloat16)


def far_shift(n_tp):
    return n_tp // 2


def spreads(packed, slots, b_refs):
    out = []
    base = 0
    for b_ref in b_refs:
        out.append(unfold_low(packed, slots, base, b_ref.shape[0]))
        base += b_ref.shape[0] // R
    return out


def slice_kernel(section, n_tp, n_b, sec_ref, *refs):
    low_refs = refs[:n_tp]
    slot_ref, gain_ref, near_ref, far_ref, h_ref, held_ref = refs[n_tp : n_tp + 6]
    b_refs = refs[n_tp + 6 : n_tp + 6 + n_b]
    h_out, *m_refs, x_all = refs[n_tp + 6 + n_b :]
    tokens, width = h_ref.shape
    far = far_shift(n_tp)
    part = width // 4

    @pl.when(sec_ref[0] != section)
    def _():
        h_out[...] = held_ref[...]

    @pl.when(sec_ref[0] == section)
    def _():
        packed = low_refs[0][...].astype(jnp.float32)
        for low_ref in low_refs[1:]:
            packed = packed + low_ref[...].astype(jnp.float32)
        rounded = packed.astype(jnp.bfloat16)
        low = spreads(rounded.astype(jnp.float32), slot_ref[...], b_refs)
        square = jnp.zeros((tokens, 1), jnp.float32)
        for c in range(4):
            span = slice(c * part, (c + 1) * part)
            h = add_delta(low, b_refs, h_ref[:, span], span)
            h_out[:, span] = h
            h = h.astype(jnp.float32)
            square = square + jnp.sum(h * h, axis=1, keepdims=True)
            lane = pl.multiple_of(sec_ref[1] * width + c * part, part)
            gain = gain_ref[:, pl.ds(lane, part)].astype(jnp.float32)
            x_all[:, span] = (h * gain).astype(jnp.bfloat16)
        square = jnp.transpose(jnp.broadcast_to(square, (tokens, HD)))[:16]
        high = square.astype(jnp.bfloat16).astype(jnp.float32)
        upper = lax.broadcasted_iota(jnp.int32, (16, HD), 0) < 8
        tail = jnp.where(upper, high, square - high).astype(jnp.bfloat16)
        for s in range(n_tp):
            if s == far:
                rows = far_ref[...]
            else:
                place = s - (s > far)
                rows = near_ref[place * width : (place + 1) * width, :]
            proj = jnp.dot(x_all[...], rows, preferred_element_type=jnp.float32)
            m_refs[s][:tokens, :] = proj.astype(jnp.bfloat16)
            m_refs[s][tokens:, :HD] = tail
            m_refs[s][tokens:, HD:] = jnp.zeros_like(tail)


def section_slice(section, n_tp, sec, lows, slots, gain, near, far, h_prev, held, b_blocks):
    tokens, width = h_prev.shape
    operands = [sec, *lows, slots, gain, near, far, h_prev, held, *b_blocks]
    return pl.pallas_call(
        functools.partial(slice_kernel, section, n_tp, len(b_blocks)),
        in_specs=[SM] + [VM] * (len(operands) - 1),
        out_specs=(VM,) * (1 + n_tp),
        out_shape=(
            sds((tokens, width), jnp.bfloat16),
            *[sds((tokens + 16, 2 * HD), jnp.bfloat16)] * n_tp,
        ),
        scratch_shapes=[pltpu.VMEM((tokens, width), jnp.bfloat16)],
        compiler_params=vmem(*b_blocks),
        cost_estimate=cost(5),
        name="section_slice_%d" % section,
    )(*operands)


def result_kernel(last, n_tp, n_b, sec_ref, back_ref, *refs):
    low_refs = refs[:n_tp]
    slot_ref, h_ref = refs[n_tp : n_tp + 2]
    b_refs = refs[n_tp + 2 : n_tp + 2 + n_b]
    out_ref = refs[n_tp + 2 + n_b]

    @pl.when(sec_ref[0] != last)
    def _():
        out_ref[0] = back_ref[...]

    @pl.when(sec_ref[0] == last)
    def _():
        packed = low_refs[0][...].astype(jnp.float32)
        for low_ref in low_refs[1:]:
            packed = packed + low_ref[...].astype(jnp.float32)
        rounded = packed.astype(jnp.bfloat16).astype(jnp.float32)
        slots = slot_ref[...]
        low = spreads(rounded, slots, b_refs)
        part = h_ref.shape[1] // 4
        for c in range(4):
            span = slice(c * part, (c + 1) * part)
            out_ref[0, :, span] = add_delta(low, b_refs, h_ref[:, span], span)


def section_result(last, n_tp, sec, back, lows, slots, held, b_blocks):
    operands = [sec, back, *lows, slots, held, *b_blocks]
    return pl.pallas_call(
        functools.partial(result_kernel, last, n_tp, len(b_blocks)),
        in_specs=[SM] + [VM] * (len(operands) - 1),
        out_specs=VM,
        out_shape=sds((1, *held.shape), jnp.bfloat16),
        compiler_params=vmem(*b_blocks),
        cost_estimate=cost(3),
        name="section_result",
    )(*operands)


def insert_kernel(new_ref, old_ref, out_ref, spot_ref):
    count = old_ref.shape[0]
    tokens = new_ref.shape[0] - count
    rows = lax.broadcasted_iota(jnp.int32, (PAGE, tokens), 0).astype(jnp.float32)
    spot_ref[...] = new_ref[tokens:, :HD].astype(jnp.float32)

    def insert(i, _):
        hit = jnp.where(spot_ref[pl.ds(i, 1), :] == rows, 1.0, 0.0)
        fresh = jnp.sum(hit, axis=1, keepdims=True) > 0.0
        hit = hit.astype(jnp.bfloat16)
        values = jnp.dot(hit, new_ref[:tokens, :], preferred_element_type=jnp.float32)
        for part in range(2):
            value = values[:, part * HD : (part + 1) * HD]
            old = old_ref[i, part].astype(jnp.float32)
            out_ref[0, i, part] = jnp.where(fresh, value, old).astype(jnp.bfloat16)
        return 0

    lax.fori_loop(0, count, insert, 0, unroll=4)


def insert_new(fresh, old):
    return pl.pallas_call(
        insert_kernel,
        in_specs=[VM] * 2,
        out_specs=VM,
        out_shape=sds((1, *old.shape), jnp.bfloat16),
        scratch_shapes=[pltpu.VMEM((old.shape[0], HD), jnp.float32)],
        compiler_params=vmem(),
        cost_estimate=cost(3),
        name="insert_new",
    )(fresh, old)


def body(
    hidden,
    queries,
    norm_gain,
    kv_weight,
    adapter_in,
    adapter_out,
    kv_pages,
    adapter_ids,
    owner_rows,
    page_table,
    lengths,
    moves,
):
    n_sec, n_req, n_tp = (lax.axis_size(a) for a in ("pipe", "req", "tp"))
    section, my_req, my_tp = (lax.axis_index(a) for a in ("pipe", "req", "tp"))
    tokens, width = hidden.shape
    depth = width * n_tp
    adapters = adapter_in.shape[1]
    q_width = queries.shape[2]

    def around(x, shift, sections=range(n_sec)):
        pairs = [
            (l * n_tp + t, l * n_tp + (t + shift) % n_tp) for l in sections for t in range(n_tp)
        ]
        return lax.ppermute(x, ("pipe", "tp"), pairs)

    def onward(x, shift, step=1, sections=range(n_sec)):
        pairs = [
            (l * n_tp + t, (l + step) % n_sec * n_tp + (t + shift) % n_tp)
            for l in sections
            for t in range(n_tp)
        ]
        return lax.ppermute(x, ("pipe", "tp"), pairs)

    def partner(x, sections=range(n_sec), step=0):
        pairs = [
            (l * n_req + i, (l + step) % n_sec * n_req + (i ^ 1))
            for l in sections
            for i in range(n_req)
        ]
        return lax.ppermute(x, ("pipe", "req"), pairs)

    def gather(x):
        return [x, partner(x)] if paired else [lax.all_gather(x, "req", axis=0, tiled=True)]

    def after(x, *others):
        return lax.optimization_barrier((x, *others))[0]

    paired = n_req == 2
    assert tokens == HD and moves.shape[0] == 16
    later = list(range(1, n_sec))
    sec = jnp.stack([section, my_tp, my_req % 2, my_req]).astype(jnp.int32)

    a_own = adapter_in[0].reshape(adapters * R, q_width)
    b_own = adapter_out[0].reshape(adapters * R, width)
    raw = kv_weight[0].reshape(2 * depth, HD)
    half = width // 2
    final = n_sec - 1
    sent = parcels(sec, hidden, raw, n_tp)
    far = far_shift(n_tp)
    turns = [s for s in range(1, n_tp) if s != far]
    detour = n_sec // 2
    passing = around(hidden, far, [detour])
    mine = {s: around(sent[s - 1], s) for s in turns}
    mine[far] = around(sent[far - 1], far, [1])
    rows_in = [hidden] + [mine[s] for s in range(1, n_tp)]
    rows_in[far] = onward(passing, 0, n_sec - detour, [detour])
    mine_late = around(after(sent[far - 1], *[mine[s] for s in turns]), far, later[1:])
    a_blocks = gather(a_own)
    b_blocks = gather(b_own)
    acc, lse, line, slots, cos, sin, leaving, spots = local_work(
        paired,
        adapters,
        sec,
        page_table.reshape(-1),
        lengths,
        adapter_ids,
        owner_rows,
        moves.reshape(-1),
        queries[0],
        kv_pages[0],
    )
    if paired:
        ready = after(b_own, lse)
        before = [onward(x, 0, 1, range(final)) for x in (ready, b_blocks[1])]
    else:
        before = [onward(b_blocks[0], 0)]
    chunks = [(0, lambda sec, i=i: i, lambda sec, i=i: i) for i in range(2 * n_tp)]
    weights = split_parts(
        sec,
        [after(raw, lse, *a_blocks, *b_blocks)],
        chunks,
        lambda section: section == 0,
        half,
        "split_first",
    )
    other = {s: partner(after(mine[s], lse), later) for s in turns}
    weights = after(weights, *other.values(), mine_late)

    shared = [queries[0], cos, sin, acc, lse, line, spots]
    n_a = len(a_blocks)
    fresh, low = attend_call(
        functools.partial(first_kernel, n_tp, n_a),
        [sec, *rows_in, weights, norm_gain, *shared],
        a_blocks,
        tokens,
        q_width,
        "first_section",
    )
    other[far] = partner(mine[far], [1])
    other_late = partner(mine_late, later[1:])
    chunks = [(0, lambda sec, i=i: 2 * sec[1] + i, lambda sec, i=i: i) for i in range(2)]
    raws = [after(raw, low)]
    for place, s in enumerate(turns, 1):
        chunks.append((len(raws), lambda sec: 0, lambda sec, p=place: 2 * p + sec[2]))
        chunks.append((len(raws) + 1, lambda sec: 0, lambda sec, p=place: 2 * p + 1 - sec[2]))
        raws += [mine[s], other[s]]
    inner = lambda section: section > 0
    near_rows = split_parts(sec, raws, chunks, inner, half, "split_near")
    chunks = [(0, lambda sec: 0, lambda sec: sec[2]), (1, lambda sec: 0, lambda sec: 1 - sec[2])]
    far_rows = split_parts(
        sec, [mine[far], other[far]], chunks, lambda section: section == 1, half, "split_far"
    )
    far_late = split_parts(
        sec, [mine_late, other_late], chunks, lambda section: section > 1, half, "split_far_late"
    )
    h_prev = h_new = hidden
    for l in later:
        lows = [onward(low, s, 1, [l - 1]) for s in range(n_tp)]
        if l == 2 and paired:
            leaving = partner(after(leaving, low))
        h_new, *parts = section_slice(
            l,
            n_tp,
            sec,
            lows,
            slots,
            norm_gain,
            near_rows,
            far_rows if l == 1 else far_late,
            h_prev,
            h_new,
            before,
        )
        parts = [parts[0]] + [around(parts[s], -s) for s in range(1, n_tp)]
        if l < final:
            h_prev = onward(after(h_new, *parts[1:]), 0)
        else:
            back = onward(after(h_new, *parts[1:]), 0, -1)
        fresh, low = attend_call(
            functools.partial(later_kernel, l, n_tp, n_a, depth),
            [sec, fresh, *parts, *shared],
            a_blocks,
            tokens,
            q_width,
            "section_%d" % l,
        )
    lows = [low] + [around(low, s) for s in range(1, n_tp)]
    if paired:
        arrived = insert_new(partner(fresh), leaving)
    else:
        leaving = insert_new(fresh, leaving)[0]
        count = moves.shape[0]
        free_slots = (n_req - 1) * ((count + n_req - 2) // (n_req - 1))
        received, dest_in, spots_in = (
            lax.all_gather(x, "req", axis=0, tiled=True)
            for x in (leaving, moves[:, 0], moves[:, 2])
        )
        target = jnp.where(dest_in == my_req, spots_in, free_slots)
        empty = jnp.zeros((free_slots, *leaving.shape[1:]), jnp.bfloat16)
        arrived = empty.at[target].set(received, mode="drop")[None]
    section_out = section_result(final, n_tp, sec, back, lows, slots, h_new, b_blocks)
    return (section_out, fresh[:tokens].reshape(1, tokens, 2, HD), arrived)


def solution(mesh):
    in_specs = (
        P("req", "tp"),
        P("pipe", "req", "tp"),
        P("pipe", None),
        P("pipe", None, None, "tp"),
        P("pipe", "req", None, "tp"),
        P("pipe", "req", None, "tp"),
        P("pipe", "req", None, None, "tp"),
        P("req"),
        P(),
        P("req", None),
        P("req"),
        P("req", None),
    )
    out_specs = (
        P("pipe", "req", "tp"),
        P("pipe", "req", None, "tp"),
        P("pipe", "req", None, None, "tp"),
    )
    return jax.shard_map(body, mesh=mesh, in_specs=in_specs, out_specs=out_specs, check_vma=False)
```
